256 devices in a mesh: crops: 8 (over y, x_lo), protos: 32 (over x_hi, z, core).
Axes of the slice: x: 4 (x_hi: 2, x_lo: 2; x = x_hi * 2 + x_lo), y: 4, z: 8, core: 2. Of those that a mesh axis runs over, the one named last changes fastest.
Arguments:
- teacher_feats: bfloat16 [4096, 384], P(('crops', 'protos')), may hold values from -6 to 6
- student_feats: bfloat16 [4096, 384], P(('crops', 'protos')), may hold values from -6 to 6
- proto_weight: float32 [384, 131072], P(None, 'protos')
Outputs:
- weight_grad: float32 [384, 131072], P('crops', 'protos')
- row_loss: float32 [4096], P(('crops', 'protos'))
The draws below stay inside these ranges and needn't reach their ends.
All inputs are finite; a program needn't handle non-finite values.
Results may differ from the reference program's by a relative error of at most 0.00066.
Values may be sent and summed in bfloat16 or wider, within the bound.
No kernel may reach another device: no remote copies, remote signals or barrier semaphores. Data moves between devices by JAX's collectives and lax.ppermute only.
A program may use at most 128 MiB of HBM per device.

```python
import math
import jax
import jax.numpy as jnp
from jax import lax

D = 384
PROTOS = 131072
ITERS = 3
CROPS = 4096
LOSS_SCALE = 8192
N_PROTOS = 32


def common_direction(key):
    signs = jax.random.randint(key, (D,), 0, 2).astype(jnp.float32)
    return (2.0 * signs - 1.0) / math.sqrt(D)


def shared_rows(key, strength, noise):
    direction = common_direction(key)
    return jnp.clip(noise + strength * direction[None, :], -6.0, 6.0).astype(jnp.bfloat16)


def shared_columns(key, top, noise):
    direction = common_direction(key)
    ramp = top * (jnp.arange(PROTOS, dtype=jnp.float32) + 0.5) / PROTOS
    return (noise + direction[:, None] * ramp[None, :]).astype(jnp.float32)


def draw_teacher_feats(key, part):
    base = key
    key = jax.random.fold_in(key, 37)
    jitter_key = jax.random.fold_in(key, 1)
    tilt_key = jax.random.fold_in(key, 2)
    tilt_share = jax.random.uniform(tilt_key, (CROPS, 1), jnp.float32, -1.0, 1.0)
    jitter = jax.random.normal(jitter_key, (CROPS, D), jnp.float32)
    return shared_rows(base, 2.0 * math.sqrt(D) * tilt_share, jitter)


def draw_student_feats(key, part):
    base = key
    key = jax.random.fold_in(key, 11)
    noise = jax.random.normal(key, (CROPS, D), jnp.float32)
    return shared_rows(base, math.sqrt(D), noise)


def draw_proto_weight(key, part):
    base = key
    key = jax.random.fold_in(key, 23)
    noise = jax.random.normal(key, (D, PROTOS), jnp.float32) / math.sqrt(D)
    return shared_columns(base, 1.5, noise)


def setup_inputs(seed: int = 0) -> dict:
    key_list = jax.random.split(jax.random.key(seed), 4)
    return {
        "teacher_feats": draw_teacher_feats(jax.random.fold_in(key_list[3], 71), 0),
        "student_feats": draw_student_feats(jax.random.fold_in(key_list[3], 71), 0),
        "proto_weight": draw_proto_weight(jax.random.fold_in(key_list[3], 71), 0),
    }


def unit_rows(values):
    wide = values.astype(jnp.float32)
    return (wide * lax.rsqrt(lax.optimization_barrier(jnp.sum(wide * wide, axis=1, keepdims=True)) + 1e-06)).astype(jnp.bfloat16)

def reference(teacher_feats, student_feats, proto_weight):
    teacher_unit = unit_rows(teacher_feats)
    student_unit = unit_rows(student_feats)
    inverse_norm = lax.rsqrt(lax.optimization_barrier(jnp.sum(proto_weight * proto_weight, axis=0)) + 1e-06)
    column_unit = proto_weight * inverse_norm[None, :]
    proto_unit = column_unit.astype(jnp.bfloat16)
    nblocks = N_PROTOS
    width = PROTOS // nblocks
    blocks = proto_unit.reshape(D, nblocks, width).transpose(1, 0, 2)

    def teacher_block(block):
        return jnp.exp(jnp.dot(teacher_unit, block, preferred_element_type=jnp.float32) / 0.07)
    row_scale = jnp.ones((CROPS,), jnp.float32)
    col_scale = jnp.ones((nblocks, width), jnp.float32)
    for step in range(ITERS):
        weighted = lax.map(lambda block: jnp.dot(row_scale, teacher_block(block), precision=lax.Precision.HIGHEST), blocks)
        col_scale = col_scale / (PROTOS * (col_scale * weighted))
        partial_rows = lax.map(lambda pair: jnp.dot(teacher_block(pair[0]), pair[1], precision=lax.Precision.HIGHEST), (blocks, col_scale))
        row_scale = row_scale / (CROPS * (row_scale * lax.optimization_barrier(jnp.sum(partial_rows, axis=0))))

    def student_block(block):
        return jnp.dot(student_unit, block, preferred_element_type=jnp.float32) / 0.1
    totals = lax.map(lambda block: lax.optimization_barrier(jnp.sum(jnp.exp(student_block(block)), axis=1)), blocks)
    log_total = jnp.log(lax.optimization_barrier(jnp.sum(totals, axis=0)))

    def final_block(pair):
        block, scales = pair
        targets = CROPS * teacher_block(block) * row_scale[:, None] * scales[None, :]
        logits = student_block(block)
        logit_grad = (LOSS_SCALE * (jnp.exp(logits - log_total[:, None]) - targets) / 0.1).astype(jnp.bfloat16)
        unit_grad = jnp.dot(student_unit.T, logit_grad, preferred_element_type=jnp.float32)
        return (unit_grad, lax.optimization_barrier(jnp.sum(targets * logits, axis=1)))
    grads, cross = lax.map(final_block, (blocks, col_scale))
    unit_grad = grads.transpose(1, 0, 2).reshape(D, PROTOS)
    row_loss = log_total - lax.optimization_barrier(jnp.sum(cross, axis=0))
    inner = lax.optimization_barrier(jnp.sum(column_unit * unit_grad, axis=0))
    weight_grad = (unit_grad - column_unit * inner[None, :]) * inverse_norm[None, :]
    return (weight_grad, row_loss)
```

```python
import math

import jax
import jax.numpy as jnp
from jax import lax
from jax.experimental import pallas as pl
from jax.experimental.pallas import tpu as pltpu
from jax.sharding import PartitionSpec as P

D = 384
PROTOS = 131072
CROPS = 4096
LOSS_SCALE = 8192
LANES = 128
MIB = 1 << 20
F32 = jnp.float32
BF16 = jnp.bfloat16
HIGHEST = lax.Precision.HIGHEST
TEACHER = math.log2(math.e) / 0.07
STUDENT = 1.0 / 0.1
LOG2E = math.log2(math.e)
VMEM = pl.BlockSpec(memory_space=pltpu.VMEM)
SMEM = pl.BlockSpec(memory_space=pltpu.SMEM)
HBM = pl.BlockSpec(memory_space=pltpu.HBM)


def params(mib=24):
    return pltpu.CompilerParams(vmem_limit_bytes=mib * MIB)


def pinned(x):
    return pltpu.with_memory_space_constraint(x, pltpu.VMEM)


def in_hbm(x):
    return pltpu.with_memory_space_constraint(x, pltpu.HBM)


def cost(flops=0, read=0, exps=0):
    return pl.CostEstimate(flops=int(flops), bytes_accessed=int(read), transcendentals=int(exps))


def unit(values):
    wide = values.astype(F32)
    return (wide * lax.rsqrt(jnp.sum(wide * wide, axis=1, keepdims=True) + 1e-6)).astype(BF16)


def own_kernel(teacher, student, out):
    rows = jnp.concatenate([unit(teacher[...]), unit(student[...])], axis=1)
    for k in range(out.shape[0]):
        out[k] = rows


def prep_kernel(weight, units, inverse, held, sems):
    blocks = held.shape[0]
    width = held.shape[2]
    copies = []
    for k in range(blocks):
        copy = pltpu.make_async_copy(weight.at[:, pl.ds(k * width, width)], held.at[k], sems.at[k])
        copy.start()
        copies.append(copy)
    for k in range(blocks):
        copies[k].wait()
        total = jnp.zeros((8, width), F32)
        for d in range(0, D, 8):
            part = held[k, d : d + 8, :]
            total += part * part
        inv = lax.rsqrt(jnp.sum(total, axis=0, keepdims=True) + 1e-6)
        inverse[:, k * width : (k + 1) * width] = inv
        for d in range(0, D, 16):
            units[d : d + 16, k * width : (k + 1) * width] = (held[k, d : d + 16, :] * inv).astype(BF16)


def col_rows(total, sums, start):
    for t in range(sums.shape[1] // LANES):
        total[start + t : start + t + 1, :] = sums[:, t * LANES : (t + 1) * LANES]


def exp_kernel(where, mine, other, units, table, student, out, total):
    core = where[0]
    half = mine.shape[0]
    first = pl.multiple_of(core * half, half)
    second = pl.multiple_of((1 - core) * half, half)
    student[pl.ds(first, half), :] = mine[:, D:]
    student[pl.ds(second, half), :] = other[:, D:]
    width = 512
    for k in range(table.shape[1] // width):
        cols = slice(k * width, (k + 1) * width)
        sums = jnp.zeros((8, width), F32)
        for start, rows in ((first, mine), (second, other)):
            e = jnp.exp2(
                jnp.dot(rows[:, :D], units[:, cols], preferred_element_type=F32) * TEACHER
            )
            table[pl.ds(start, half), cols] = e
            for d in range(0, half, 8):
                sums += e[d : d + 8, :]
        col_rows(total, jnp.sum(sums, axis=0, keepdims=True), k * width // LANES)
    every = total[...]
    for k in range(out.shape[0]):
        out[k] = every


def col_scales(parts, scale):
    scale[...] = 1.0 / (PROTOS * jnp.sum(parts[...], axis=0))


def lane_sums(acc):
    ones = jnp.ones((8, LANES), F32)
    sums = lax.dot_general(
        ones, acc, (((1,), (1,)), ((), ())), precision=HIGHEST, preferred_element_type=F32
    )
    return sums[0:1, :]


def row_kernel(table, parts, out, scale, acc, total):
    col_scales(parts, scale)
    rows, cols = table.shape
    step = 64
    for i in range(0, rows, step):
        sums = jnp.zeros((step, LANES), F32)
        for j in range(cols // LANES):
            sums += table[i : i + step, j * LANES : (j + 1) * LANES] * scale[j : j + 1, :]
        acc[i : i + step, :] = sums
    col_rows(total, lane_sums(acc[...]), 0)
    every = total[...]
    for k in range(out.shape[0]):
        out[k] = every


def down(vector):
    return jnp.transpose(jnp.broadcast_to(vector, (LANES, LANES)))


def col_kernel(table, parts, out, weight, total):
    rows, cols = table.shape
    scale = 1.0 / (CROPS * jnp.sum(parts[...], axis=0))
    for t in range(rows // LANES):
        weight[t * LANES : (t + 1) * LANES, :] = down(scale[t : t + 1, :])
    tiles = 8
    for j in range(0, cols, tiles * LANES):
        sums = [jnp.zeros((8, LANES), F32) for _ in range(tiles)]
        for i in range(0, rows, 8):
            w = weight[i : i + 8, :]
            for t in range(tiles):
                sums[t] += table[i : i + 8, j + t * LANES : j + (t + 1) * LANES] * w
        for t in range(tiles):
            row = j // LANES + t
            total[row : row + 1, :] = jnp.sum(sums[t], axis=0, keepdims=True)
    every = total[...]
    for k in range(out.shape[0]):
        out[k] = every


def last_kernel(table, parts, student, units, out, scale, acc, total):
    col_scales(parts, scale)
    rows, cols = table.shape
    acc[...] = jnp.zeros_like(acc)
    width = 512
    step = 256
    for k in range(0, cols, width):
        for i in range(0, rows, step):
            z = jnp.dot(
                student[i : i + step, :], units[:, k : k + width], preferred_element_type=F32
            )
            z = z * STUDENT
            x = jnp.exp2(z * LOG2E)
            plain = cross = exps = None
            for t in range(width // LANES):
                j = k // LANES + t
                here = slice(t * LANES, (t + 1) * LANES)
                e = table[i : i + step, j * LANES : (j + 1) * LANES] * scale[j : j + 1, :]
                zt, xt = z[:, here], x[:, here]
                plain = e if t == 0 else plain + e
                cross = e * zt if t == 0 else cross + e * zt
                exps = xt if t == 0 else exps + xt
            acc[0, i : i + step, :] += plain
            acc[1, i : i + step, :] += cross
            acc[2, i : i + step, :] += exps
    total[...] = jnp.zeros_like(total)
    for n in range(3):
        col_rows(total, lane_sums(acc[n]), n * rows // LANES)
    every = total[...]
    for k in range(out.shape[0]):
        out[k] = every


def loss_kernel(parts, out, loss):
    sums = jnp.sum(parts[...], axis=0)
    n = loss.shape[0]
    plain, cross, exps = (sums[k * n : (k + 1) * n, :] for k in range(3))
    loss[...] = jnp.log(exps) - cross / plain
    every = jnp.concatenate(
        [(LOSS_SCALE / 0.1) / exps, (LOSS_SCALE / 0.1) / plain], axis=0
    )
    for k in range(out.shape[0]):
        out[k] = every


def grad_kernel(
    where, mine, other, units, weight, inverse, scale, factors, out,
    held, wsub, punit, csub, grad, sems, wsem,
):
    core, place = where[0], where[1]
    groups = factors.shape[0]
    width = wsub.shape[1]
    half = mine.shape[0] // groups
    begin = pl.multiple_of(place * width, width)
    wcopy = pltpu.make_async_copy(weight.at[:, pl.ds(begin, width)], wsub, wsem)
    wcopy.start()

    def piece(g, side):
        src = (mine, other)[side]
        return pltpu.make_async_copy(
            src.at[pl.ds(g * half, half), :],
            held.at[side, pl.ds(g * half, half), :],
            sems.at[side, g],
        )

    for g in range(groups):
        for side in range(2):
            piece(g, side).start()
    punit[...] = units[:, pl.ds(begin, width)]
    inv = inverse[:, pl.ds(begin, width)]
    tiles = width // LANES
    for t in range(tiles):
        csub[:, t * LANES : (t + 1) * LANES] = scale[pl.ds(place * tiles + t, 1), :]
    grad[...] = jnp.zeros_like(grad)
    chunks = half // LANES

    def body(g, carry):
        for side in range(2):
            piece(g, side).wait()
            number = core if side == 0 else 1 - core
            rows = held[side, pl.ds(pl.multiple_of(g * half, half), half), :]
            t_rows, s_rows = rows[:, :D], rows[:, D:]
            zt = jnp.dot(t_rows, punit[...], preferred_element_type=F32)
            zs = jnp.dot(s_rows, punit[...], preferred_element_type=F32)
            a = jnp.concatenate(
                [down(factors[g, pl.ds(number * chunks + n, 1), :]) for n in range(chunks)], axis=0
            )
            b = jnp.concatenate(
                [down(factors[g, pl.ds((2 + number) * chunks + n, 1), :]) for n in range(chunks)],
                axis=0,
            )
            parts = []
            for t in range(tiles):
                here = slice(t * LANES, (t + 1) * LANES)
                e = jnp.exp2(zt[:, here] * TEACHER) * (csub[:, here] * b)
                x = jnp.exp2(zs[:, here] * (STUDENT * LOG2E)) * a
                parts.append((x - e).astype(BF16))
            logit_grad = jnp.concatenate(parts, axis=1)
            grad[...] += lax.dot_general(
                s_rows, logit_grad, (((0,), (0,)), ((), ())), preferred_element_type=F32
            )
        return carry

    lax.fori_loop(0, groups, body, 0)
    wcopy.wait()
    inner = jnp.zeros((8, width), F32)
    for d in range(0, D, 8):
        inner += wsub[d : d + 8, :] * inv * grad[d : d + 8, :]
    inner = jnp.sum(inner, axis=0, keepdims=True)
    share = out.shape[1]
    for d in range(0, D, 8):
        cu = wsub[d : d + 8, :] * inv
        out[d // share, d % share : d % share + 8, :] = (grad[d : d + 8, :] - cu * inner) * inv


def struct(shape, dtype=F32):
    return jax.ShapeDtypeStruct(shape, dtype)


def local(teacher_feats, student_feats, proto_weight):
    crops, protos = lax.axis_size("crops"), lax.axis_size("protos")
    own = teacher_feats.shape[0]
    rows = own * protos
    half = rows // 2
    cols = proto_weight.shape[1]
    width = cols // crops
    share = D // crops
    ctile, rtile = cols // LANES, rows // LANES
    number = lax.axis_index("protos")
    place = lax.axis_index("crops")
    where = jnp.stack([number % 2, place]).astype(jnp.int32)
    swap = [(j, j ^ 1) for j in range(protos)]
    same_core = [[j for j in range(protos) if j % 2 == core] for core in range(2)]

    copies = pl.pallas_call(
        own_kernel,
        out_shape=struct((protos // 2, own, 2 * D), BF16),
        in_specs=[VMEM, VMEM],
        out_specs=VMEM,
    )(teacher_feats, student_feats)
    mine = lax.all_to_all(
        copies, "protos", 0, 0, tiled=True, axis_index_groups=same_core
    ).reshape(half, 2 * D)
    other = lax.ppermute(mine, "protos", swap)
    all_mine = lax.all_gather(mine, "crops", axis=0, tiled=True)

    units, inverse = pl.pallas_call(
        prep_kernel,
        out_shape=(pltpu.VMEM((D, cols), BF16), pltpu.VMEM((1, cols), F32)),
        in_specs=[HBM],
        out_specs=(VMEM, VMEM),
        scratch_shapes=[pltpu.VMEM((8, D, cols // 8), F32), pltpu.SemaphoreType.DMA((8,))],
        compiler_params=params(),
        cost_estimate=cost(3 * D * cols, 4 * D * cols),
    )(in_hbm(proto_weight))

    table, student, parts = pl.pallas_call(
        exp_kernel,
        out_shape=(
            pltpu.VMEM((rows, cols), F32),
            pltpu.VMEM((rows, D), BF16),
            struct((crops, ctile, LANES)),
        ),
        in_specs=[SMEM, VMEM, VMEM, VMEM],
        out_specs=(VMEM, VMEM, VMEM),
        scratch_shapes=[pltpu.VMEM((ctile, LANES), F32)],
        compiler_params=params(),
        cost_estimate=cost(2 * rows * D * cols, 0, rows * cols),
    )(where, mine, other, pinned(units))

    def over_crops(x):
        return lax.all_to_all(x, "crops", 0, 0, tiled=True)

    def over_protos(x):
        return lax.all_to_all(x, "protos", 0, 0, tiled=True)

    for step in range(2):
        rparts, _ = pl.pallas_call(
            row_kernel,
            out_shape=(struct((protos, rtile, LANES)), struct((ctile, LANES))),
            in_specs=[VMEM, VMEM],
            out_specs=(VMEM, VMEM),
            scratch_shapes=[pltpu.VMEM((rows, LANES), F32), pltpu.VMEM((rtile, LANES), F32)],
            compiler_params=params(),
            cost_estimate=cost(2 * rows * cols),
        )(pinned(table), over_crops(parts))
        parts = pl.pallas_call(
            col_kernel,
            out_shape=struct((crops, ctile, LANES)),
            in_specs=[VMEM, VMEM],
            out_specs=VMEM,
            scratch_shapes=[pltpu.VMEM((rows, LANES), F32), pltpu.VMEM((ctile, LANES), F32)],
            compiler_params=params(),
            cost_estimate=cost(2 * rows * cols),
        )(pinned(table), over_protos(rparts))

    rparts, scale = pl.pallas_call(
        last_kernel,
        out_shape=(struct((protos, 4 * rtile, LANES)), struct((ctile, LANES))),
        in_specs=[VMEM, VMEM, VMEM, VMEM],
        out_specs=(VMEM, VMEM),
        scratch_shapes=[pltpu.VMEM((3, rows, LANES), F32), pltpu.VMEM((4 * rtile, LANES), F32)],
        compiler_params=params(),
        cost_estimate=cost(2 * rows * D * cols, 0, rows * cols),
    )(pinned(table), over_crops(parts), pinned(student), pinned(units))

    all_mine, rparts = lax.optimization_barrier((all_mine, rparts))
    all_other = lax.ppermute(all_mine, "protos", swap)
    factors, loss = pl.pallas_call(
        loss_kernel,
        out_shape=(struct((crops, 2 * rtile, LANES)), struct((rtile, LANES))),
        in_specs=[VMEM],
        out_specs=(VMEM, VMEM),
    )(over_protos(rparts))
    first = (number % 2) * half + (number // 2) * own
    row_loss = lax.dynamic_slice(loss.reshape(rows), (first,), (own,))

    grad = pl.pallas_call(
        grad_kernel,
        out_shape=struct((crops, share, width)),
        in_specs=[SMEM, HBM, HBM, VMEM, HBM, VMEM, VMEM, VMEM],
        out_specs=VMEM,
        scratch_shapes=[
            pltpu.VMEM((2, crops * half, 2 * D), BF16),
            pltpu.VMEM((D, width), F32),
            pltpu.VMEM((D, width), BF16),
            pltpu.VMEM((1, width), F32),
            pltpu.VMEM((D, width), F32),
            pltpu.SemaphoreType.DMA((2, crops)),
            pltpu.SemaphoreType.DMA,
        ],
        compiler_params=params(),
        cost_estimate=cost(6 * CROPS * D * width, 0, 2 * CROPS * width),
    )(
        where, in_hbm(all_mine), in_hbm(all_other), pinned(units), in_hbm(proto_weight),
        pinned(inverse), scale, over_crops(factors),
    )
    moved = lax.all_to_all(grad, "crops", 0, 0, tiled=True)
    weight_grad = moved.transpose(1, 0, 2).reshape(share, cols)
    return (weight_grad, row_loss)


def solution(mesh):
    placed = (P(("crops", "protos"), None), P(("crops", "protos"), None), P(None, "protos"))
    return jax.shard_map(
        local,
        mesh=mesh,
        in_specs=placed,
        out_specs=(P("crops", "protos"), P(("crops", "protos"))),
        check_vma=False,
    )
```

```python
import functools
import math

import jax
import jax.numpy as jnp
from jax import lax
from jax.experimental import pallas as pl
from jax.experimental.pallas import tpu as pltpu
from jax.sharding import PartitionSpec as P

D = 384
PROTOS = 131072
CROPS = 4096
LOSS_SCALE = 8192
LANES = 128
MIB = 1 << 20
F32 = jnp.float32
BF16 = jnp.bfloat16
HIGHEST = lax.Precision.HIGHEST
TEACHER = math.log2(math.e) / 0.07
STUDENT = 1.0 / 0.1
LOG2E = math.log2(math.e)
VMEM = pl.BlockSpec(memory_space=pltpu.VMEM)
SMEM = pl.BlockSpec(memory_space=pltpu.SMEM)
HBM = pl.BlockSpec(memory_space=pltpu.HBM)


def params(mib=14):
    return pltpu.CompilerParams(vmem_limit_bytes=mib * MIB)


def pinned(x):
    return pltpu.with_memory_space_constraint(x, pltpu.VMEM)


def in_hbm(x):
    return pltpu.with_memory_space_constraint(x, pltpu.HBM)


def cost(flops=0, read=0, exps=0):
    return pl.CostEstimate(flops=int(flops), bytes_accessed=int(read), transcendentals=int(exps))


def unit(values):
    wide = values.astype(F32)
    return (wide * lax.rsqrt(jnp.sum(wide * wide, axis=1, keepdims=True) + 1e-6)).astype(BF16)


def own_kernel(teacher, student, out, held, sems):
    copies = [
        pltpu.make_async_copy(x, held.at[n], sems.at[n]) for n, x in enumerate((teacher, student))
    ]
    for copy in copies:
        copy.start()
    for copy in copies:
        copy.wait()
    rows = jnp.concatenate([unit(held[0]), unit(held[1])], axis=1)
    for k in range(out.shape[0]):
        out[k] = rows


def prep_kernel(where, weight, units, inverse, share, held, sems):
    blocks = held.shape[0]
    width = held.shape[2]
    copies = []
    for k in range(blocks):
        copy = pltpu.make_async_copy(weight.at[:, pl.ds(k * width, width)], held.at[k], sems.at[k])
        copy.start()
        copies.append(copy)
    for k in range(blocks):
        copies[k].wait()
        total = jnp.zeros((8, width), F32)
        for d in range(0, D, 8):
            part = held[k, d : d + 8, :]
            total += part * part
        inv = lax.rsqrt(jnp.sum(total, axis=0, keepdims=True) + 1e-6)
        inverse[:, k * width : (k + 1) * width] = inv
        for d in range(0, D, 16):
            units[d : d + 16, k * width : (k + 1) * width] = (held[k, d : d + 16, :] * inv).astype(BF16)
    count = share.shape[0]
    begin = pl.multiple_of(where[1] * count, count)
    share[...] = jnp.transpose(units[:, pl.ds(begin, count)])


def col_rows(total, sums, start):
    for t in range(sums.shape[1] // LANES):
        total[start + t : start + t + 1, :] = sums[:, t * LANES : (t + 1) * LANES]


def exp_rows(rows, start, units, table, student, total):
    half = rows.shape[0]
    student[pl.ds(start, half), :] = rows[:, D:]
    width = 512
    for k in range(table.shape[1] // width):
        cols = slice(k * width, (k + 1) * width)
        e = jnp.exp2(jnp.dot(rows[:, :D], units[:, cols], preferred_element_type=F32) * TEACHER)
        table[pl.ds(start, half), cols] = e
        sums = e[0:8, :]
        for d in range(8, half, 8):
            sums += e[d : d + 8, :]
        col_rows(total, jnp.sum(sums, axis=0, keepdims=True), k * width // LANES)


def exp_mine_kernel(where, mine, units, table, student, total, held, sem):
    copy = pltpu.make_async_copy(mine, held, sem)
    copy.start()
    copy.wait()
    half = held.shape[0]
    exp_rows(held, pl.multiple_of(where[0] * half, half), units, table, student, total)


def exp_other_kernel(where, other, units, first, _, __, table, student, out, total):
    half = other.shape[0]
    exp_rows(other, pl.multiple_of((1 - where[0]) * half, half), units, table, student, total)
    every = first[...] + total[...]
    for k in range(out.shape[0]):
        out[k] = every


def col_scales(parts, scale):
    scale[...] = 1.0 / (PROTOS * jnp.sum(parts[...], axis=0))


def lane_sums(acc):
    ones = jnp.ones((8, LANES), F32)
    sums = lax.dot_general(
        ones, acc, (((1,), (1,)), ((), ())), precision=HIGHEST, preferred_element_type=F32
    )
    return sums[0:1, :]


def row_kernel(table, parts, out, scale, acc, total):
    col_scales(parts, scale)
    rows, cols = table.shape
    step = 64
    for i in range(0, rows, step):
        sums = jnp.zeros((step, LANES), F32)
        for j in range(cols // LANES):
            sums += table[i : i + step, j * LANES : (j + 1) * LANES] * scale[j : j + 1, :]
        acc[i : i + step, :] = sums
    col_rows(total, lane_sums(acc[...]), 0)
    every = total[...]
    for k in range(out.shape[0]):
        out[k] = every


def down(vector):
    return jnp.transpose(jnp.broadcast_to(vector, (LANES, LANES)))


def col_kernel(table, parts, out, weight, total):
    rows, cols = table.shape
    scale = 1.0 / (CROPS * jnp.sum(parts[...], axis=0))
    for t in range(rows // LANES):
        weight[t * LANES : (t + 1) * LANES, :] = down(scale[t : t + 1, :])
    tiles = 8
    for j in range(0, cols, tiles * LANES):
        sums = [jnp.zeros((8, LANES), F32) for _ in range(tiles)]
        for i in range(0, rows, 8):
            w = weight[i : i + 8, :]
            for t in range(tiles):
                sums[t] += table[i : i + 8, j + t * LANES : j + (t + 1) * LANES] * w
        for t in range(tiles):
            row = j // LANES + t
            total[row : row + 1, :] = jnp.sum(sums[t], axis=0, keepdims=True)
    every = total[...]
    for k in range(out.shape[0]):
        out[k] = every


def last_kernel(table, parts, student, units, out, scale, acc):
    col_scales(parts, scale)
    rows, cols = table.shape
    acc[...] = jnp.zeros_like(acc)
    width = 512
    step = 256
    for k in range(0, cols, width):
        for i in range(0, rows, step):
            z = jnp.dot(
                student[i : i + step, :], units[:, k : k + width], preferred_element_type=F32
            )
            x = jnp.exp2(z * (STUDENT * LOG2E))
            plain = cross = exps = None
            for t in range(width // LANES):
                j = k // LANES + t
                here = slice(t * LANES, (t + 1) * LANES)
                e = table[i : i + step, j * LANES : (j + 1) * LANES] * scale[j : j + 1, :]
                zt, xt = z[:, here], x[:, here]
                plain = e if t == 0 else plain + e
                cross = e * zt if t == 0 else cross + e * zt
                exps = xt if t == 0 else exps + xt
            acc[0, i : i + step, :] += plain
            acc[1, i : i + step, :] += cross
            acc[2, i : i + step, :] += exps
    every = jnp.concatenate([lane_sums(acc[0]), lane_sums(acc[2])], axis=1)
    cross = lane_sums(acc[1]) * STUDENT
    count = out.shape[0]
    own = rows // count
    for k in range(count):
        tile = first_crop(k, rows // 2, own) // LANES
        out[k, :, : 2 * rows] = every
        out[k, :, 2 * rows :] = cross[:, tile * LANES : (tile + 1) * LANES]


def first_crop(number, half, own):
    return (number & 1) * half + (number >> 1) * own


def loss_kernel(where, parts, out, loss, held):
    sums = parts[0]
    for k in range(1, parts.shape[0]):
        sums += parts[k]
    rows = out.shape[2] // 2
    held[...] = sums
    first = where[2]
    tile = pl.multiple_of(first // LANES * LANES, LANES)
    plain = held[:, pl.ds(tile, LANES)]
    exps = held[:, pl.ds(rows + tile, LANES)]
    row = jnp.log(exps) - sums[:, 2 * rows :] / plain
    loss[...] = pltpu.roll(row, (LANES - first % LANES) % LANES, 1)[:, : loss.shape[1]]
    every = (LOSS_SCALE / 0.1) / sums[:, : 2 * rows]
    for k in range(out.shape[0]):
        out[k] = every


def grad_kernel(
    order, where, mine, other, units, weight, inverse, scale, factors, out,
    held, logits, wsub, csub, turned, grad, sems, wsem,
):
    core, place = where[0], where[1]
    groups = factors.shape[0]
    rows = factors.shape[2] // 2
    width = wsub.shape[1]
    half = mine.shape[0] // groups
    begin = pl.multiple_of(place * width, width)
    copies = []
    for n in range(groups):
        here = pl.ds(n * half, half)
        copies.append(pltpu.make_async_copy(mine.at[here, :], held.at[here, :], sems.at[n]))
        copies[-1].start()
    wcopy = pltpu.make_async_copy(weight.at[:, pl.ds(begin, width)], wsub, wsem)
    wcopy.start()
    inv = inverse[:, pl.ds(begin, width)]
    tiles = width // LANES
    for t in range(tiles):
        csub[t * LANES : (t + 1) * LANES, :] = down(scale[pl.ds(place * tiles + t, 1), :])
    nt = (((1,), (1,)), ((), ()))
    last = 2 * groups

    def crops_of(c, here):
        n = c % groups
        return (other if c < groups else held)[n * half : (n + 1) * half, here]

    def products(c):
        for k in range(2):
            logits[c % 2, k] = lax.dot_general(
                units[...], crops_of(c, slice(k * D, (k + 1) * D)), nt, preferred_element_type=F32
            )

    products(0)
    for c in range(last):
        if c + 1 == groups:
            for copy in copies:
                copy.wait()
        if c + 1 < last:
            products(c + 1)
        owner = 1 - core if c < groups else core
        group = order[c % groups]
        parts = []
        for t in range(0, half, LANES):
            at = pl.multiple_of(owner * half, half) + t
            a = factors[group, :, pl.ds(at, LANES)]
            b = factors[group, :, pl.ds(rows + at, LANES)]
            here = slice(t, t + LANES)
            x = jnp.exp2(logits[c % 2, 1, :, here] * (STUDENT * LOG2E)) * b
            e = jnp.exp2(logits[c % 2, 0, :, here] * TEACHER) * (csub[...] * a)
            parts.append((x - e).astype(BF16))
        part = jnp.dot(
            jnp.concatenate(parts, axis=1),
            crops_of(c, slice(D, 2 * D)),
            preferred_element_type=F32,
        )
        turned[...] = part if c == 0 else turned[...] + part
    for t in range(tiles):
        for d in range(0, D, LANES):
            grad[d : d + LANES, t * LANES : (t + 1) * LANES] = jnp.transpose(
                turned[t * LANES : (t + 1) * LANES, d : d + LANES]
            )
    wcopy.wait()
    inner = jnp.zeros((8, width), F32)
    for d in range(0, D, 8):
        inner += wsub[d : d + 8, :] * inv * grad[d : d + 8, :]
    inner = jnp.sum(inner, axis=0, keepdims=True)
    share = out.shape[1]
    for d in range(0, D, 8):
        cu = wsub[d : d + 8, :] * inv
        out[d // share, d % share : d % share + 8, :] = (grad[d : d + 8, :] - cu * inner) * inv


def struct(shape, dtype=F32):
    return jax.ShapeDtypeStruct(shape, dtype)


def local(teacher_feats, student_feats, proto_weight):
    crops, protos = lax.axis_size("crops"), lax.axis_size("protos")
    own = teacher_feats.shape[0]
    rows = own * protos
    half = rows // 2
    cols = proto_weight.shape[1]
    width = cols // crops
    share = D // crops
    ctile, rtile = cols // LANES, rows // LANES
    number = lax.axis_index("protos")
    place = lax.axis_index("crops")
    first = first_crop(number, half, own)
    where = jnp.stack([number & 1, place, first]).astype(jnp.int32)
    swap = [(j, j ^ 1) for j in range(protos)]
    same_core = [[j for j in range(protos) if j % 2 == core] for core in range(2)]
    ring = list(range(0, crops, 2)) + list(range(crops - 1, 0, -2))

    def over_crops(x):
        return lax.all_to_all(x, "crops", 0, 0, tiled=True)

    def over_protos(x):
        return lax.all_to_all(x, "protos", 0, 0, tiled=True)

    copies = pl.pallas_call(
        own_kernel,
        out_shape=pltpu.VMEM((protos // 2, own, 2 * D), BF16),
        in_specs=[HBM, HBM],
        out_specs=VMEM,
        scratch_shapes=[pltpu.VMEM((2, own, D), BF16), pltpu.SemaphoreType.DMA((2,))],
        compiler_params=params(),
        cost_estimate=cost(rows * D, 2 * rows * D),
    )(in_hbm(teacher_feats), in_hbm(student_feats))
    mine = lax.all_to_all(
        copies, "protos", 0, 0, tiled=True, axis_index_groups=same_core
    ).reshape(half, 2 * D)

    units, inverse, share_units = pl.pallas_call(
        prep_kernel,
        out_shape=(
            pltpu.VMEM((D, cols), BF16),
            pltpu.VMEM((1, cols), F32),
            pltpu.VMEM((width, D), BF16),
        ),
        in_specs=[SMEM, HBM],
        out_specs=(VMEM, VMEM, VMEM),
        scratch_shapes=[pltpu.VMEM((8, D, cols // 8), F32), pltpu.SemaphoreType.DMA((8,))],
        compiler_params=params(),
        cost_estimate=cost(3 * D * cols, 4 * D * cols),
    )(where, in_hbm(proto_weight))
    mine, inverse = lax.optimization_barrier((mine, inverse))
    other = lax.ppermute(mine, "protos", swap)
    all_mine = lax.all_gather(mine, "crops", axis=0, tiled=True, axis_index_groups=[ring])

    table, student, total = pl.pallas_call(
        exp_mine_kernel,
        out_shape=(
            pltpu.VMEM((rows, cols), F32),
            pltpu.VMEM((rows, D), BF16),
            pltpu.VMEM((ctile, LANES), F32),
        ),
        in_specs=[SMEM, HBM, VMEM],
        out_specs=(VMEM, VMEM, VMEM),
        scratch_shapes=[pltpu.VMEM((half, 2 * D), BF16), pltpu.SemaphoreType.DMA],
        compiler_params=params(),
        cost_estimate=cost(rows * D * cols, 0, rows * cols // 2),
    )(where, in_hbm(mine), pinned(units))
    table, student, parts = pl.pallas_call(
        exp_other_kernel,
        out_shape=(
            pltpu.VMEM((rows, cols), F32),
            pltpu.VMEM((rows, D), BF16),
            struct((crops, ctile, LANES)),
        ),
        in_specs=[SMEM] + [VMEM] * 5,
        out_specs=(VMEM, VMEM, VMEM),
        input_output_aliases={4: 0, 5: 1},
        scratch_shapes=[pltpu.VMEM((ctile, LANES), F32)],
        compiler_params=params(),
        cost_estimate=cost(rows * D * cols, 0, rows * cols // 2),
    )(where, other, pinned(units), pinned(total), pinned(table), pinned(student))

    for step in range(2):
        rparts, _ = pl.pallas_call(
            row_kernel,
            out_shape=(struct((protos, rtile, LANES)), struct((ctile, LANES))),
            in_specs=[VMEM, VMEM],
            out_specs=(VMEM, VMEM),
            scratch_shapes=[pltpu.VMEM((rows, LANES), F32), pltpu.VMEM((rtile, LANES), F32)],
            compiler_params=params(),
            cost_estimate=cost(2 * rows * cols),
        )(pinned(table), over_crops(parts))
        parts = pl.pallas_call(
            col_kernel,
            out_shape=struct((crops, ctile, LANES)),
            in_specs=[VMEM, VMEM],
            out_specs=VMEM,
            scratch_shapes=[pltpu.VMEM((rows, LANES), F32), pltpu.VMEM((ctile, LANES), F32)],
            compiler_params=params(),
            cost_estimate=cost(2 * rows * cols),
        )(pinned(table), over_protos(rparts))

    rparts, scale = pl.pallas_call(
        last_kernel,
        out_shape=(struct((protos, 1, 2 * rows + LANES)), struct((ctile, LANES))),
        in_specs=[VMEM, VMEM, VMEM, VMEM],
        out_specs=(VMEM, VMEM),
        scratch_shapes=[pltpu.VMEM((3, rows, LANES), F32)],
        compiler_params=params(),
        cost_estimate=cost(2 * rows * D * cols, 0, rows * cols),
    )(pinned(table), over_crops(parts), pinned(student), pinned(units))
    all_mine, rparts = lax.optimization_barrier((all_mine, rparts))
    all_other = lax.ppermute(all_mine, "protos", swap)
    factors, loss = pl.pallas_call(
        loss_kernel,
        out_shape=(pltpu.VMEM((crops, 1, 2 * rows), F32), struct((1, own))),
        in_specs=[SMEM, VMEM],
        out_specs=(VMEM, VMEM),
        scratch_shapes=[pltpu.VMEM((1, 2 * rows + LANES), F32)],
        compiler_params=params(),
    )(where, over_protos(rparts))

    grad = pl.pallas_call(
        functools.partial(grad_kernel, ring),
        out_shape=pltpu.VMEM((crops, share, width), F32),
        in_specs=[SMEM, HBM, VMEM, VMEM, HBM, VMEM, VMEM, VMEM],
        out_specs=VMEM,
        scratch_shapes=[
            pltpu.VMEM((crops * half, 2 * D), BF16),
            pltpu.VMEM((2, 2, width, half), F32),
            pltpu.VMEM((D, width), F32),
            pltpu.VMEM((width, LANES), F32),
            pltpu.VMEM((width, D), F32),
            pltpu.VMEM((D, width), F32),
            pltpu.SemaphoreType.DMA((crops,)),
            pltpu.SemaphoreType.DMA,
        ],
        compiler_params=params(20),
        cost_estimate=cost(6 * CROPS * D * width, 0, 2 * CROPS * width),
    )(
        where, in_hbm(all_mine), pinned(all_other), pinned(share_units), in_hbm(proto_weight),
        pinned(inverse), scale, over_crops(factors),
    )
    moved = over_crops(grad)
    weight_grad = moved.transpose(1, 0, 2).reshape(share, cols)
    return (weight_grad, loss.reshape(own))


def solution(mesh):
    placed = (P(("crops", "protos"), None), P(("crops", "protos"), None), P(None, "protos"))
    return jax.shard_map(
        local,
        mesh=mesh,
        in_specs=placed,
        out_specs=(P("crops", "protos"), P(("crops", "protos"))),
        check_vma=False,
    )
```

```python
import functools
import math

import jax
import jax.numpy as jnp
from jax import lax
from jax.experimental import pallas as pl
from jax.experimental.pallas import tpu as pltpu
from jax.sharding import PartitionSpec as P

D = 384
PROTOS = 131072
CROPS = 4096
LOSS_SCALE = 8192
LANES = 128
MIB = 1 << 20
F32 = jnp.float32
BF16 = jnp.bfloat16
SPARE = 16
HIGHEST = lax.Precision.HIGHEST
TEACHER = math.log2(math.e) / 0.07
STUDENT = 1.0 / 0.1
LOG2E = math.log2(math.e)
VMEM = pl.BlockSpec(memory_space=pltpu.VMEM)
SMEM = pl.BlockSpec(memory_space=pltpu.SMEM)
HBM = pl.BlockSpec(memory_space=pltpu.HBM)


def params(mib=14):
    return pltpu.CompilerParams(vmem_limit_bytes=mib * MIB)


def pinned(x):
    return pltpu.with_memory_space_constraint(x, pltpu.VMEM)


def in_hbm(x):
    return pltpu.with_memory_space_constraint(x, pltpu.HBM)


def cost(flops=0, read=0, exps=0):
    return pl.CostEstimate(flops=int(flops), bytes_accessed=int(read), transcendentals=int(exps))


def unit(values):
    wide = values.astype(F32)
    return (wide * lax.rsqrt(jnp.sum(wide * wide, axis=1, keepdims=True) + 1e-6)).astype(BF16)


def own_kernel(teacher, student, out, held, sems):
    copies = [
        pltpu.make_async_copy(x, held.at[n], sems.at[n]) for n, x in enumerate((teacher, student))
    ]
    for copy in copies:
        copy.start()
    for copy in copies:
        copy.wait()
    rows = jnp.concatenate([unit(held[0]), unit(held[1])], axis=1)
    for k in range(out.shape[0]):
        out[k] = rows


def prep_kernel(weight, units, inverse, held, sems):
    blocks = held.shape[0]
    width = held.shape[2]
    copies = []
    for k in range(blocks):
        copy = pltpu.make_async_copy(weight.at[:, pl.ds(k * width, width)], held.at[k], sems.at[k])
        copy.start()
        copies.append(copy)
    for k in range(blocks):
        copies[k].wait()
        total = jnp.zeros((8, width), F32)
        for d in range(0, D, 8):
            part = held[k, d : d + 8, :]
            total += part * part
        inv = lax.rsqrt(jnp.sum(total, axis=0, keepdims=True) + 1e-6)
        inverse[:, k * width : (k + 1) * width] = inv
        for d in range(0, D, 16):
            units[d : d + 16, k * width : (k + 1) * width] = (held[k, d : d + 16, :] * inv).astype(BF16)

def col_rows(total, sums, start):
    for t in range(sums.shape[1] // LANES):
        total[start + t : start + t + 1, :] = sums[:, t * LANES : (t + 1) * LANES]


def exp_rows(rows, start, units, table, student, total):
    half = rows.shape[0]
    student[pl.ds(start, half), :] = rows[:, D:]
    width = 512
    for k in range(table.shape[1] // width):
        cols = slice(k * width, (k + 1) * width)
        e = jnp.exp2(jnp.dot(rows[:, :D], units[:D, cols], preferred_element_type=F32) * TEACHER)
        table[pl.ds(start, half), cols] = e
        sums = e[0:8, :]
        for d in range(8, half, 8):
            sums += e[d : d + 8, :]
        col_rows(total, jnp.sum(sums, axis=0, keepdims=True), k * width // LANES)


def exp_mine_kernel(where, mine, units, table, student, total, held, sem):
    copy = pltpu.make_async_copy(mine, held, sem)
    copy.start()
    copy.wait()
    half = held.shape[0]
    exp_rows(held, pl.multiple_of(where[0] * half, half), units, table, student, total)


def exp_other_kernel(where, other, units, first, _, __, table, student, out, total):
    half = other.shape[0]
    exp_rows(other, pl.multiple_of((1 - where[0]) * half, half), units, table, student, total)
    every = first[...] + total[...]
    for k in range(out.shape[0]):
        out[k] = every


def col_scales(parts, scale):
    scale[...] = 1.0 / (PROTOS * jnp.sum(parts[...], axis=0))


def lane_sums(acc):
    ones = jnp.ones((8, LANES), F32)
    sums = lax.dot_general(
        ones, acc, (((1,), (1,)), ((), ())), precision=HIGHEST, preferred_element_type=F32
    )
    return sums[0:1, :]


def row_kernel(table, parts, out, scale, acc, total):
    col_scales(parts, scale)
    rows, cols = table.shape
    step = 64
    for i in range(0, rows, step):
        sums = jnp.zeros((step, LANES), F32)
        for j in range(cols // LANES):
            sums += table[i : i + step, j * LANES : (j + 1) * LANES] * scale[j : j + 1, :]
        acc[i : i + step, :] = sums
    col_rows(total, lane_sums(acc[...]), 0)
    every = total[...]
    for k in range(out.shape[0]):
        out[k] = every


def down(vector):
    return jnp.transpose(jnp.broadcast_to(vector, (LANES, LANES)))


def col_kernel(table, parts, out, weight, total):
    rows, cols = table.shape
    scale = 1.0 / (CROPS * jnp.sum(parts[...], axis=0))
    for t in range(rows // LANES):
        weight[t * LANES : (t + 1) * LANES, :] = down(scale[t : t + 1, :])
    tiles = 8
    for j in range(0, cols, tiles * LANES):
        sums = [jnp.zeros((8, LANES), F32) for _ in range(tiles)]
        for i in range(0, rows, 8):
            w = weight[i : i + 8, :]
            for t in range(tiles):
                sums[t] += table[i : i + 8, j + t * LANES : j + (t + 1) * LANES] * w
        for t in range(tiles):
            row = j // LANES + t
            total[row : row + 1, :] = jnp.sum(sums[t], axis=0, keepdims=True)
    every = total[...]
    for k in range(out.shape[0]):
        out[k] = every


def last_kernel(table, parts, student, units, out, scale, acc):
    col_scales(parts, scale)
    rows, cols = table.shape
    acc[...] = jnp.zeros_like(acc)
    width = 512
    step = 256
    for k in range(0, cols, width):
        for i in range(0, rows, step):
            z = jnp.dot(
                student[i : i + step, :], units[:D, k : k + width], preferred_element_type=F32
            )
            x = jnp.exp2(z * (STUDENT * LOG2E))
            plain = cross = exps = None
            for t in range(width // LANES):
                j = k // LANES + t
                here = slice(t * LANES, (t + 1) * LANES)
                e = table[i : i + step, j * LANES : (j + 1) * LANES] * scale[j : j + 1, :]
                zt, xt = z[:, here], x[:, here]
                plain = e if t == 0 else plain + e
                cross = e * zt if t == 0 else cross + e * zt
                exps = xt if t == 0 else exps + xt
            acc[0, i : i + step, :] += plain
            acc[1, i : i + step, :] += cross
            acc[2, i : i + step, :] += exps
    every = jnp.concatenate([lane_sums(acc[0]), lane_sums(acc[2])], axis=1)
    cross = lane_sums(acc[1]) * STUDENT
    count = out.shape[0]
    own = rows // count
    for k in range(count):
        tile = first_crop(k, rows // 2, own) // LANES
        out[k, :, : 2 * rows] = every
        out[k, :, 2 * rows :] = cross[:, tile * LANES : (tile + 1) * LANES]


def first_crop(number, half, own):
    return (number & 1) * half + (number >> 1) * own


def factor_kernel(where, parts, out, loss, sums):
    total = parts[0]
    for k in range(1, parts.shape[0]):
        total += parts[k]
    sums[...] = total
    rows = out.shape[2] // 2
    every = (LOSS_SCALE / 0.1) / total[:, : 2 * rows]
    for k in range(out.shape[0]):
        out[k] = every
    first = where[2]
    tile = pl.multiple_of(first // LANES * LANES, LANES)
    plain = sums[:, pl.ds(tile, LANES)]
    exps = sums[:, pl.ds(rows + tile, LANES)]
    row = jnp.log(exps) - total[:, 2 * rows :] / plain
    loss[...] = pltpu.roll(row, (LANES - first % LANES) % LANES, 1)[:, : loss.shape[1]]


def grad_kernel(
    order, where, mine, other, units, weight, inverse, scale, factors, own, out, loss,
    held, logits, wsub, punit, csub, turned, grad, sems, wsem, lsem,
):
    core, place = where[0], where[1]
    lcopy = pltpu.make_async_copy(own, loss, lsem)
    lcopy.start()
    groups = factors.shape[0]
    rows = factors.shape[2] // 2
    width = wsub.shape[1]
    half = mine.shape[0] // groups
    begin = pl.multiple_of(place * width, width)
    copies = []
    for n in range(groups):
        here = pl.ds(n * half, half)
        copies.append(pltpu.make_async_copy(mine.at[here, :], held.at[here, :], sems.at[n]))
        copies[-1].start()
    wcopy = pltpu.make_async_copy(weight.at[:, pl.ds(begin, width)], wsub, wsem)
    wcopy.start()
    punit[...] = jnp.transpose(units[:D, pl.ds(begin, width)])
    inv = inverse[:, pl.ds(begin, width)]
    tiles = width // LANES
    for t in range(tiles):
        csub[t * LANES : (t + 1) * LANES, :] = down(scale[pl.ds(place * tiles + t, 1), :])
    nt = (((1,), (1,)), ((), ()))
    last = 2 * groups

    def crops_of(c, here):
        n = c % groups
        return (other if c < groups else held)[n * half : (n + 1) * half, here]

    def products(c):
        for k in range(2):
            logits[c % 2, k] = lax.dot_general(
                punit[...], crops_of(c, slice(k * D, (k + 1) * D)), nt, preferred_element_type=F32
            )

    products(0)
    for c in range(last):
        if c + 1 == groups:
            for copy in copies:
                copy.wait()
        if c + 1 < last:
            products(c + 1)
        owner = 1 - core if c < groups else core
        group = order[c % groups]
        parts = []
        for t in range(0, half, LANES):
            at = pl.multiple_of(owner * half, half) + t
            a = factors[group, :, pl.ds(at, LANES)]
            b = factors[group, :, pl.ds(rows + at, LANES)]
            here = slice(t, t + LANES)
            x = jnp.exp2(logits[c % 2, 1, :, here] * (STUDENT * LOG2E)) * b
            e = jnp.exp2(logits[c % 2, 0, :, here] * TEACHER) * (csub[...] * a)
            parts.append((x - e).astype(BF16))
        part = jnp.dot(
            jnp.concatenate(parts, axis=1),
            crops_of(c, slice(D, 2 * D)),
            preferred_element_type=F32,
        )
        turned[...] = part if c == 0 else turned[...] + part
    for t in range(tiles):
        for d in range(0, D, LANES):
            grad[d : d + LANES, t * LANES : (t + 1) * LANES] = jnp.transpose(
                turned[t * LANES : (t + 1) * LANES, d : d + LANES]
            )
    wcopy.wait()
    inner = jnp.zeros((8, width), F32)
    for d in range(0, D, 8):
        inner += wsub[d : d + 8, :] * inv * grad[d : d + 8, :]
    inner = jnp.sum(inner, axis=0, keepdims=True)
    share = out.shape[1]
    for d in range(0, D, 8):
        cu = wsub[d : d + 8, :] * inv
        out[d // share, d % share : d % share + 8, :] = (grad[d : d + 8, :] - cu * inner) * inv
    lcopy.wait()


def struct(shape, dtype=F32):
    return jax.ShapeDtypeStruct(shape, dtype)


def local(teacher_feats, student_feats, proto_weight):
    crops, protos = lax.axis_size("crops"), lax.axis_size("protos")
    own = teacher_feats.shape[0]
    rows = own * protos
    half = rows // 2
    cols = proto_weight.shape[1]
    width = cols // crops
    share = D // crops
    ctile, rtile = cols // LANES, rows // LANES
    number = lax.axis_index("protos")
    place = lax.axis_index("crops")
    first = first_crop(number, half, own)
    where = jnp.stack([number & 1, place, first]).astype(jnp.int32)
    swap = [(j, j ^ 1) for j in range(protos)]
    group = [
        [
            (2 * y + (pair ^ (j >= protos // 2))) * protos + j
            for j in range(protos)
        ]
        for y in range(crops // 2)
        for pair in range(2)
    ]
    same_core = [g[core::2] for g in group for core in range(2)]
    both = ("crops", "protos")
    ring = list(range(0, crops, 2)) + list(range(crops - 1, 0, -2))

    def over_crops(x):
        return lax.all_to_all(x, "crops", 0, 0, tiled=True)

    def over_group(x):
        return lax.all_to_all(x, both, 0, 0, tiled=True, axis_index_groups=group)

    copies = pl.pallas_call(
        own_kernel,
        out_shape=pltpu.VMEM((protos // 2, own, 2 * D), BF16),
        in_specs=[HBM, HBM],
        out_specs=VMEM,
        scratch_shapes=[pltpu.VMEM((2, own, D), BF16), pltpu.SemaphoreType.DMA((2,))],
        compiler_params=params(),
        cost_estimate=cost(rows * D, 2 * rows * D),
    )(in_hbm(teacher_feats), in_hbm(student_feats))
    mine = lax.all_to_all(
        copies, both, 0, 0, tiled=True, axis_index_groups=same_core
    ).reshape(half, 2 * D)

    units, inverse = pl.pallas_call(
        prep_kernel,
        out_shape=(
            pltpu.VMEM((D + SPARE, cols), BF16),
            pltpu.VMEM((1, cols), F32),
        ),
        in_specs=[HBM],
        out_specs=(VMEM, VMEM),
        scratch_shapes=[pltpu.VMEM((8, D, cols // 8), F32), pltpu.SemaphoreType.DMA((8,))],
        compiler_params=params(),
        cost_estimate=cost(3 * D * cols, 4 * D * cols),
    )(in_hbm(proto_weight))
    mine, inverse, where = lax.optimization_barrier((mine, inverse, where))
    other = lax.ppermute(mine, "protos", swap)
    all_mine = lax.all_gather(mine, "crops", axis=0, tiled=True, axis_index_groups=[ring])

    table, student, total = pl.pallas_call(
        exp_mine_kernel,
        out_shape=(
            pltpu.VMEM((rows, cols), F32),
            pltpu.VMEM((rows, D), BF16),
            pltpu.VMEM((ctile, LANES), F32),
        ),
        in_specs=[SMEM, HBM, VMEM],
        out_specs=(VMEM, VMEM, VMEM),
        scratch_shapes=[pltpu.VMEM((half, 2 * D), BF16), pltpu.SemaphoreType.DMA],
        compiler_params=params(),
        cost_estimate=cost(rows * D * cols, 0, rows * cols // 2),
    )(where, in_hbm(mine), pinned(units))
    table, student, parts = pl.pallas_call(
        exp_other_kernel,
        out_shape=(
            pltpu.VMEM((rows, cols), F32),
            pltpu.VMEM((rows, D), BF16),
            struct((crops, ctile, LANES)),
        ),
        in_specs=[SMEM] + [VMEM] * 5,
        out_specs=(VMEM, VMEM, VMEM),
        input_output_aliases={4: 0, 5: 1},
        scratch_shapes=[pltpu.VMEM((ctile, LANES), F32)],
        compiler_params=params(),
        cost_estimate=cost(rows * D * cols, 0, rows * cols // 2),
    )(where, other, pinned(units), pinned(total), pinned(table), pinned(student))

    for step in range(2):
        rparts, _ = pl.pallas_call(
            row_kernel,
            out_shape=(struct((protos, rtile, LANES)), struct((ctile, LANES))),
            in_specs=[VMEM, VMEM],
            out_specs=(VMEM, VMEM),
            scratch_shapes=[pltpu.VMEM((rows, LANES), F32), pltpu.VMEM((rtile, LANES), F32)],
            compiler_params=params(),
            cost_estimate=cost(2 * rows * cols),
        )(pinned(table), over_crops(parts))
        parts = pl.pallas_call(
            col_kernel,
            out_shape=struct((crops, ctile, LANES)),
            in_specs=[VMEM, VMEM],
            out_specs=VMEM,
            scratch_shapes=[pltpu.VMEM((rows, LANES), F32), pltpu.VMEM((ctile, LANES), F32)],
            compiler_params=params(),
            cost_estimate=cost(2 * rows * cols),
        )(pinned(table), over_group(rparts))

    rparts, scale = pl.pallas_call(
        last_kernel,
        out_shape=(struct((protos, 1, 2 * rows + LANES)), struct((ctile, LANES))),
        in_specs=[VMEM, VMEM, VMEM, VMEM],
        out_specs=(VMEM, VMEM),
        scratch_shapes=[pltpu.VMEM((3, rows, LANES), F32)],
        compiler_params=params(),
        cost_estimate=cost(2 * rows * D * cols, 0, rows * cols),
    )(pinned(table), over_crops(parts), pinned(student), pinned(units))
    all_mine, rparts = lax.optimization_barrier((all_mine, rparts))
    all_other = lax.ppermute(all_mine, "protos", swap)
    factors, loss = pl.pallas_call(
        factor_kernel,
        out_shape=(pltpu.VMEM((crops, 1, 2 * rows), F32), pltpu.VMEM((1, own), F32)),
        in_specs=[SMEM, VMEM],
        out_specs=(VMEM, VMEM),
        scratch_shapes=[pltpu.VMEM((1, 2 * rows + LANES), F32)],
        compiler_params=params(),
    )(where, over_group(rparts))

    grad, loss = pl.pallas_call(
        functools.partial(grad_kernel, ring),
        out_shape=(pltpu.VMEM((crops, share, width), F32), pltpu.HBM((1, own), F32)),
        in_specs=[SMEM, HBM, VMEM, VMEM, HBM, VMEM, VMEM, VMEM, VMEM],
        out_specs=(VMEM, HBM),
        scratch_shapes=[
            pltpu.VMEM((crops * half, 2 * D), BF16),
            pltpu.VMEM((2, 2, width, half), F32),
            pltpu.VMEM((D, width), F32),
            pltpu.VMEM((width, D), BF16),
            pltpu.VMEM((width, LANES), F32),
            pltpu.VMEM((width, D), F32),
            pltpu.VMEM((D, width), F32),
            pltpu.SemaphoreType.DMA((crops,)),
            pltpu.SemaphoreType.DMA,
            pltpu.SemaphoreType.DMA,
        ],
        compiler_params=params(20),
        cost_estimate=cost(6 * CROPS * D * width, 0, 2 * CROPS * width),
    )(
        where, in_hbm(all_mine), pinned(all_other), pinned(units), in_hbm(proto_weight),
        pinned(inverse), scale, over_crops(factors), pinned(loss),
    )
    moved = over_crops(grad)
    weight_grad = moved.transpose(1, 0, 2).reshape(share, cols)
    return (weight_grad, loss.reshape(own))


def solution(mesh):
    placed = (P(("crops", "protos"), None), P(("crops", "protos"), None), P(None, "protos"))
    return jax.shard_map(
        local,
        mesh=mesh,
        in_specs=placed,
        out_specs=(P("crops", "protos"), P(("crops", "protos"))),
        check_vma=False,
    )
```

```python
import functools
import math

import jax
import jax.numpy as jnp
from jax import lax
from jax.experimental import pallas as pl
from jax.experimental.pallas import tpu as pltpu
from jax.sharding import PartitionSpec as P

D = 384
PROTOS = 131072
CROPS = 4096
LOSS_SCALE = 8192
LANES = 128
MIB = 1 << 20
F32 = jnp.float32
BF16 = jnp.bfloat16
SPARE = 16
HIGHEST = lax.Precision.HIGHEST
TEACHER = math.log2(math.e) / 0.07
STUDENT = 1.0 / 0.1
LOG2E = math.log2(math.e)
VMEM = pl.BlockSpec(memory_space=pltpu.VMEM)
SMEM = pl.BlockSpec(memory_space=pltpu.SMEM)
HBM = pl.BlockSpec(memory_space=pltpu.HBM)


def params(mib=14):
    return pltpu.CompilerParams(vmem_limit_bytes=mib * MIB)


def pinned(x):
    return pltpu.with_memory_space_constraint(x, pltpu.VMEM)


def in_hbm(x):
    return pltpu.with_memory_space_constraint(x, pltpu.HBM)


def cost(flops=0, read=0, exps=0):
    return pl.CostEstimate(flops=int(flops), bytes_accessed=int(read), transcendentals=int(exps))


def unit(values):
    wide = values.astype(F32)
    return (wide * lax.rsqrt(jnp.sum(wide * wide, axis=1, keepdims=True) + 1e-6)).astype(BF16)


def own_kernel(teacher, student, out, held, sems):
    copies = [
        pltpu.make_async_copy(x, held.at[n], sems.at[n]) for n, x in enumerate((teacher, student))
    ]
    for copy in copies:
        copy.start()
    for copy in copies:
        copy.wait()
    rows = jnp.concatenate([unit(held[0]), unit(held[1])], axis=1)
    for k in range(out.shape[0]):
        out[k] = rows


def prep_kernel(weight, units, inverse, held, sems):
    blocks = held.shape[0]
    width = held.shape[2]
    copies = []
    for k in range(blocks):
        copy = pltpu.make_async_copy(weight.at[:, pl.ds(k * width, width)], held.at[k], sems.at[k])
        copy.start()
        copies.append(copy)
    for k in range(blocks):
        copies[k].wait()
        total = jnp.zeros((8, width), F32)
        for d in range(0, D, 8):
            part = held[k, d : d + 8, :]
            total += part * part
        inv = lax.rsqrt(jnp.sum(total, axis=0, keepdims=True) + 1e-6)
        inverse[:, k * width : (k + 1) * width] = inv
        for d in range(0, D, 16):
            units[d : d + 16, k * width : (k + 1) * width] = (held[k, d : d + 16, :] * inv).astype(BF16)

def col_rows(total, sums, start):
    for t in range(sums.shape[1] // LANES):
        total[start + t : start + t + 1, :] = sums[:, t * LANES : (t + 1) * LANES]


def exp_rows(rows, start, units, table, total):
    half = rows.shape[0]
    width = 512
    for k in range(table.shape[1] // width):
        cols = slice(k * width, (k + 1) * width)
        e = jnp.exp2(jnp.dot(rows[:, :D], units[:D, cols], preferred_element_type=F32) * TEACHER)
        table[pl.ds(start, half), cols] = e
        sums = e[0:8, :]
        for d in range(8, half, 8):
            sums += e[d : d + 8, :]
        col_rows(total, jnp.sum(sums, axis=0, keepdims=True), k * width // LANES)


def exp_mine_kernel(where, mine, units, table, student, total, held, sems):
    half = held.shape[0]
    start = pl.multiple_of(where[0] * half, half)
    copies = [
        pltpu.make_async_copy(mine.at[:, pl.ds(0, D)], held, sems.at[0]),
        pltpu.make_async_copy(
            mine.at[:, pl.ds(D, D)], student.at[pl.ds(start, half), :], sems.at[1]
        ),
    ]
    for copy in copies:
        copy.start()
    copies[0].wait()
    exp_rows(held, start, units, table, total)
    copies[1].wait()


def exp_other_kernel(where, other, units, first, _, __, table, student, out, total):
    half = other.shape[0]
    start = pl.multiple_of((1 - where[0]) * half, half)
    student[pl.ds(start, half), :] = other[:, D:]
    exp_rows(other, start, units, table, total)
    every = first[...] + total[...]
    for k in range(out.shape[0]):
        out[k] = every


def col_scales(parts, scale):
    scale[...] = 1.0 / (PROTOS * jnp.sum(parts[...], axis=0))


def lane_sums(acc):
    ones = jnp.ones((8, LANES), F32)
    sums = lax.dot_general(
        ones, acc, (((1,), (1,)), ((), ())), precision=HIGHEST, preferred_element_type=F32
    )
    return sums[0:1, :]


def row_kernel(table, parts, out, scale, acc, total):
    col_scales(parts, scale)
    rows, cols = table.shape
    step = 64
    for i in range(0, rows, step):
        sums = jnp.zeros((step, LANES), F32)
        for j in range(cols // LANES):
            sums += table[i : i + step, j * LANES : (j + 1) * LANES] * scale[j : j + 1, :]
        acc[i : i + step, :] = sums
    col_rows(total, lane_sums(acc[...]), 0)
    every = total[...]
    for k in range(out.shape[0]):
        out[k] = every


def down(vector):
    return jnp.transpose(jnp.broadcast_to(vector, (LANES, LANES)))


def col_kernel(table, parts, out, weight, total):
    rows, cols = table.shape
    scale = 1.0 / (CROPS * jnp.sum(parts[...], axis=0))
    for t in range(rows // LANES):
        weight[t * LANES : (t + 1) * LANES, :] = down(scale[t : t + 1, :])
    tiles = 8
    for j in range(0, cols, tiles * LANES):
        sums = [jnp.zeros((8, LANES), F32) for _ in range(tiles)]
        for i in range(0, rows, 8):
            w = weight[i : i + 8, :]
            for t in range(tiles):
                sums[t] += table[i : i + 8, j + t * LANES : j + (t + 1) * LANES] * w
        for t in range(tiles):
            row = j // LANES + t
            total[row : row + 1, :] = jnp.sum(sums[t], axis=0, keepdims=True)
    every = total[...]
    for k in range(out.shape[0]):
        out[k] = every


def last_kernel(table, parts, student, units, out, scale, acc):
    col_scales(parts, scale)
    rows, cols = table.shape
    acc[...] = jnp.zeros_like(acc)
    width = 512
    step = 256
    for k in range(0, cols, width):
        for i in range(0, rows, step):
            z = jnp.dot(
                student[i : i + step, :], units[:D, k : k + width], preferred_element_type=F32
            )
            x = jnp.exp2(z * (STUDENT * LOG2E))
            plain = cross = exps = None
            for t in range(width // LANES):
                j = k // LANES + t
                here = slice(t * LANES, (t + 1) * LANES)
                e = table[i : i + step, j * LANES : (j + 1) * LANES] * scale[j : j + 1, :]
                zt, xt = z[:, here], x[:, here]
                plain = e if t == 0 else plain + e
                cross = e * zt if t == 0 else cross + e * zt
                exps = xt if t == 0 else exps + xt
            acc[0, i : i + step, :] += plain
            acc[1, i : i + step, :] += cross
            acc[2, i : i + step, :] += exps
    every = jnp.concatenate([lane_sums(acc[0]), lane_sums(acc[2])], axis=1)
    cross = lane_sums(acc[1]) * STUDENT
    count = out.shape[0]
    own = rows // count
    for k in range(count):
        tile = first_crop(k, rows // 2, own) // LANES
        out[k, :, : 2 * rows] = every
        out[k, :, 2 * rows :] = cross[:, tile * LANES : (tile + 1) * LANES]


def first_crop(number, half, own):
    return (number & 1) * half + (number >> 1) * own


def factor_kernel(where, parts, out, loss, sums):
    total = parts[0]
    for k in range(1, parts.shape[0]):
        total += parts[k]
    sums[...] = total
    rows = out.shape[2] // 2
    every = (LOSS_SCALE / 0.1) / total[:, : 2 * rows]
    for k in range(out.shape[0]):
        out[k] = every
    first = where[2]
    tile = pl.multiple_of(first // LANES * LANES, LANES)
    plain = sums[:, pl.ds(tile, LANES)]
    exps = sums[:, pl.ds(rows + tile, LANES)]
    row = jnp.log(exps) - total[:, 2 * rows :] / plain
    loss[...] = pltpu.roll(row, (LANES - first % LANES) % LANES, 1)[:, : loss.shape[1]]


def grad_kernel(
    order, where, mine, other, units, weight, inverse, scale, factors, own, out, loss,
    held, logits, wsub, punit, csub, turned, grad, sems, wsem, lsem,
):
    core, place = where[0], where[1]
    lcopy = pltpu.make_async_copy(own, loss, lsem)
    lcopy.start()
    groups = factors.shape[0]
    rows = factors.shape[2] // 2
    width = wsub.shape[1]
    half = mine.shape[0] // groups
    begin = pl.multiple_of(place * width, width)
    copies = []
    for n in range(groups):
        here = pl.ds(n * half, half)
        copies.append(pltpu.make_async_copy(mine.at[here, :], held.at[here, :], sems.at[n]))
        copies[-1].start()
    wcopy = pltpu.make_async_copy(weight.at[:, pl.ds(begin, width)], wsub, wsem)
    wcopy.start()
    punit[...] = jnp.transpose(units[:D, pl.ds(begin, width)])
    inv = inverse[:, pl.ds(begin, width)]
    tiles = width // LANES
    for t in range(tiles):
        csub[t * LANES : (t + 1) * LANES, :] = down(scale[pl.ds(place * tiles + t, 1), :])
    nt = (((1,), (1,)), ((), ()))
    last = 2 * groups

    def crops_of(c, here):
        n = c % groups
        return (other if c < groups else held)[n * half : (n + 1) * half, here]

    def products(c):
        for k in range(2):
            logits[c % 2, k] = lax.dot_general(
                punit[...], crops_of(c, slice(k * D, (k + 1) * D)), nt, preferred_element_type=F32
            )

    products(0)
    for c in range(last):
        if c + 1 == groups:
            for copy in copies:
                copy.wait()
        if c + 1 < last:
            products(c + 1)
        owner = 1 - core if c < groups else core
        group = order[c % groups]
        parts = []
        for t in range(0, half, LANES):
            at = pl.multiple_of(owner * half, half) + t
            a = factors[group, :, pl.ds(at, LANES)]
            b = factors[group, :, pl.ds(rows + at, LANES)]
            here = slice(t, t + LANES)
            x = jnp.exp2(logits[c % 2, 1, :, here] * (STUDENT * LOG2E)) * b
            e = jnp.exp2(logits[c % 2, 0, :, here] * TEACHER) * (csub[...] * a)
            parts.append((x - e).astype(BF16))
        part = jnp.dot(
            jnp.concatenate(parts, axis=1),
            crops_of(c, slice(D, 2 * D)),
            preferred_element_type=F32,
        )
        turned[...] = part if c == 0 else turned[...] + part
    for t in range(tiles):
        for d in range(0, D, LANES):
            grad[d : d + LANES, t * LANES : (t + 1) * LANES] = jnp.transpose(
                turned[t * LANES : (t + 1) * LANES, d : d + LANES]
            )
    wcopy.wait()
    inner = jnp.zeros((8, width), F32)
    for d in range(0, D, 8):
        inner += wsub[d : d + 8, :] * inv * grad[d : d + 8, :]
    inner = jnp.sum(inner, axis=0, keepdims=True)
    share = out.shape[1]
    for d in range(0, D, 8):
        cu = wsub[d : d + 8, :] * inv
        out[d // share, d % share : d % share + 8, :] = (grad[d : d + 8, :] - cu * inner) * inv
    lcopy.wait()


def struct(shape, dtype=F32):
    return jax.ShapeDtypeStruct(shape, dtype)


def local(teacher_feats, student_feats, proto_weight):
    crops, protos = lax.axis_size("crops"), lax.axis_size("protos")
    own = teacher_feats.shape[0]
    rows = own * protos
    half = rows // 2
    cols = proto_weight.shape[1]
    width = cols // crops
    share = D // crops
    ctile, rtile = cols // LANES, rows // LANES
    number = lax.axis_index("protos")
    place = lax.axis_index("crops")
    first = first_crop(number, half, own)
    where = jnp.stack([number & 1, place, first]).astype(jnp.int32)
    swap = [(j, j ^ 1) for j in range(protos)]
    group = [
        [
            (2 * y + (pair ^ (j >= protos // 2))) * protos + j
            for j in range(protos)
        ]
        for y in range(crops // 2)
        for pair in range(2)
    ]
    same_core = [g[core::2] for g in group for core in range(2)]
    both = ("crops", "protos")
    ring = list(range(0, crops, 2)) + list(range(crops - 1, 0, -2))

    def over_crops(x):
        return lax.all_to_all(x, "crops", 0, 0, tiled=True)

    def over_group(x):
        return lax.all_to_all(x, both, 0, 0, tiled=True, axis_index_groups=group)

    copies = pl.pallas_call(
        own_kernel,
        out_shape=pltpu.VMEM((protos // 2, own, 2 * D), BF16),
        in_specs=[HBM, HBM],
        out_specs=VMEM,
        scratch_shapes=[pltpu.VMEM((2, own, D), BF16), pltpu.SemaphoreType.DMA((2,))],
        compiler_params=params(),
        cost_estimate=cost(rows * D, 2 * rows * D),
    )(in_hbm(teacher_feats), in_hbm(student_feats))
    mine = lax.all_to_all(
        copies, both, 0, 0, tiled=True, axis_index_groups=same_core
    ).reshape(half, 2 * D)

    units, inverse = pl.pallas_call(
        prep_kernel,
        out_shape=(
            pltpu.VMEM((D + SPARE, cols), BF16),
            pltpu.VMEM((1, cols), F32),
        ),
        in_specs=[HBM],
        out_specs=(VMEM, VMEM),
        scratch_shapes=[pltpu.VMEM((8, D, cols // 8), F32), pltpu.SemaphoreType.DMA((8,))],
        compiler_params=params(),
        cost_estimate=cost(3 * D * cols, 4 * D * cols),
    )(in_hbm(proto_weight))
    mine, inverse, where = lax.optimization_barrier((mine, inverse, where))
    other = lax.ppermute(mine, "protos", swap)
    all_mine = lax.all_gather(mine, "crops", axis=0, tiled=True, axis_index_groups=[ring])

    table, student, total = pl.pallas_call(
        exp_mine_kernel,
        out_shape=(
            pltpu.VMEM((rows, cols), F32),
            pltpu.VMEM((rows, D), BF16),
            pltpu.VMEM((ctile, LANES), F32),
        ),
        in_specs=[SMEM, HBM, VMEM],
        out_specs=(VMEM, VMEM, VMEM),
        scratch_shapes=[pltpu.VMEM((half, D), BF16), pltpu.SemaphoreType.DMA((2,))],
        compiler_params=params(),
        cost_estimate=cost(rows * D * cols, 0, rows * cols // 2),
    )(where, in_hbm(mine), pinned(units))
    table, student, parts = pl.pallas_call(
        exp_other_kernel,
        out_shape=(
            pltpu.VMEM((rows, cols), F32),
            pltpu.VMEM((rows, D), BF16),
            struct((crops, ctile, LANES)),
        ),
        in_specs=[SMEM] + [VMEM] * 5,
        out_specs=(VMEM, VMEM, VMEM),
        input_output_aliases={4: 0, 5: 1},
        scratch_shapes=[pltpu.VMEM((ctile, LANES), F32)],
        compiler_params=params(),
        cost_estimate=cost(rows * D * cols, 0, rows * cols // 2),
    )(where, other, pinned(units), pinned(total), pinned(table), pinned(student))

    for step in range(2):
        rparts, _ = pl.pallas_call(
            row_kernel,
            out_shape=(struct((protos, rtile, LANES)), struct((ctile, LANES))),
            in_specs=[VMEM, VMEM],
            out_specs=(VMEM, VMEM),
            scratch_shapes=[pltpu.VMEM((rows, LANES), F32), pltpu.VMEM((rtile, LANES), F32)],
            compiler_params=params(),
            cost_estimate=cost(2 * rows * cols),
        )(pinned(table), over_crops(parts))
        parts = pl.pallas_call(
            col_kernel,
            out_shape=struct((crops, ctile, LANES)),
            in_specs=[VMEM, VMEM],
            out_specs=VMEM,
            scratch_shapes=[pltpu.VMEM((rows, LANES), F32), pltpu.VMEM((ctile, LANES), F32)],
            compiler_params=params(),
            cost_estimate=cost(2 * rows * cols),
        )(pinned(table), over_group(rparts))

    rparts, scale = pl.pallas_call(
        last_kernel,
        out_shape=(struct((protos, 1, 2 * rows + LANES)), struct((ctile, LANES))),
        in_specs=[VMEM, VMEM, VMEM, VMEM],
        out_specs=(VMEM, VMEM),
        scratch_shapes=[pltpu.VMEM((3, rows, LANES), F32)],
        compiler_params=params(),
        cost_estimate=cost(2 * rows * D * cols, 0, rows * cols),
    )(pinned(table), over_crops(parts), pinned(student), pinned(units))
    all_mine, rparts = lax.optimization_barrier((all_mine, rparts))
    all_other = lax.ppermute(all_mine, "protos", swap)
    factors, loss = pl.pallas_call(
        factor_kernel,
        out_shape=(pltpu.VMEM((crops, 1, 2 * rows), F32), pltpu.VMEM((1, own), F32)),
        in_specs=[SMEM, VMEM],
        out_specs=(VMEM, VMEM),
        scratch_shapes=[pltpu.VMEM((1, 2 * rows + LANES), F32)],
        compiler_params=params(),
    )(where, over_group(rparts))

    grad, loss = pl.pallas_call(
        functools.partial(grad_kernel, ring),
        out_shape=(pltpu.VMEM((crops, share, width), F32), pltpu.HBM((1, own), F32)),
        in_specs=[SMEM, HBM, VMEM, VMEM, HBM, VMEM, VMEM, VMEM, VMEM],
        out_specs=(VMEM, HBM),
        scratch_shapes=[
            pltpu.VMEM((crops * half, 2 * D), BF16),
            pltpu.VMEM((2, 2, width, half), F32),
            pltpu.VMEM((D, width), F32),
            pltpu.VMEM((width, D), BF16),
            pltpu.VMEM((width, LANES), F32),
            pltpu.VMEM((width, D), F32),
            pltpu.VMEM((D, width), F32),
            pltpu.SemaphoreType.DMA((crops,)),
            pltpu.SemaphoreType.DMA,
            pltpu.SemaphoreType.DMA,
        ],
        compiler_params=params(20),
        cost_estimate=cost(6 * CROPS * D * width, 0, 2 * CROPS * width),
    )(
        where, in_hbm(all_mine), pinned(all_other), pinned(units), in_hbm(proto_weight),
        pinned(inverse), scale, over_crops(factors), pinned(loss),
    )
    moved = over_crops(grad)
    weight_grad = moved.transpose(1, 0, 2).reshape(share, cols)
    return (weight_grad, loss.reshape(own))


def solution(mesh):
    placed = (P(("crops", "protos"), None), P(("crops", "protos"), None), P(None, "protos"))
    return jax.shard_map(
        local,
        mesh=mesh,
        in_specs=placed,
        out_specs=(P("crops", "protos"), P(("crops", "protos"))),
        check_vma=False,
    )
```

```python
import functools
import math

import jax
import jax.numpy as jnp
from jax import lax
from jax.experimental import pallas as pl
from jax.experimental.pallas import tpu as pltpu
from jax.sharding import PartitionSpec as P

D = 384
PROTOS = 131072
CROPS = 4096
LOSS_SCALE = 8192
LANES = 128
MIB = 1 << 20
F32 = jnp.float32
BF16 = jnp.bfloat16
SPARE = 16
HIGHEST = lax.Precision.HIGHEST
TEACHER = math.log2(math.e) / 0.07
STUDENT = 1.0 / 0.1
LOG2E = math.log2(math.e)
VMEM = pl.BlockSpec(memory_space=pltpu.VMEM)
SMEM = pl.BlockSpec(memory_space=pltpu.SMEM)
HBM = pl.BlockSpec(memory_space=pltpu.HBM)


def params(mib=14):
    return pltpu.CompilerParams(vmem_limit_bytes=mib * MIB)


def pinned(x):
    return pltpu.with_memory_space_constraint(x, pltpu.VMEM)


def in_hbm(x):
    return pltpu.with_memory_space_constraint(x, pltpu.HBM)


def cost(flops=0, read=0, exps=0):
    return pl.CostEstimate(flops=int(flops), bytes_accessed=int(read), transcendentals=int(exps))


def unit(values):
    wide = values.astype(F32)
    return (wide * lax.rsqrt(jnp.sum(wide * wide, axis=1, keepdims=True) + 1e-6)).astype(BF16)


def own_kernel(teacher, student, out, held, sems):
    copies = [
        pltpu.make_async_copy(x, held.at[n], sems.at[n]) for n, x in enumerate((teacher, student))
    ]
    for copy in copies:
        copy.start()
    for copy in copies:
        copy.wait()
    rows = jnp.concatenate([unit(held[0]), unit(held[1])], axis=1)
    for k in range(out.shape[0]):
        out[k] = rows


def prep_kernel(weight, units, inverse, held, sems):
    blocks = held.shape[0]
    width = held.shape[2]
    copies = []
    for k in range(blocks):
        copy = pltpu.make_async_copy(weight.at[:, pl.ds(k * width, width)], held.at[k], sems.at[k])
        copy.start()
        copies.append(copy)
    for k in range(blocks):
        copies[k].wait()
        total = jnp.zeros((8, width), F32)
        for d in range(0, D, 8):
            part = held[k, d : d + 8, :]
            total += part * part
        inv = lax.rsqrt(jnp.sum(total, axis=0, keepdims=True) + 1e-6)
        inverse[:, k * width : (k + 1) * width] = inv
        for d in range(0, D, 16):
            units[d : d + 16, k * width : (k + 1) * width] = (held[k, d : d + 16, :] * inv).astype(BF16)

def col_rows(total, sums, start):
    for t in range(sums.shape[1] // LANES):
        total[start + t : start + t + 1, :] = sums[:, t * LANES : (t + 1) * LANES]


def exp_rows(rows, start, units, table, total):
    half = rows.shape[0]
    width = 512
    for k in range(table.shape[1] // width):
        cols = slice(k * width, (k + 1) * width)
        e = jnp.exp2(jnp.dot(rows[:, :D], units[:D, cols], preferred_element_type=F32) * TEACHER)
        table[pl.ds(start, half), cols] = e
        sums = e[0:8, :]
        for d in range(8, half, 8):
            sums += e[d : d + 8, :]
        col_rows(total, jnp.sum(sums, axis=0, keepdims=True), k * width // LANES)


def exp_mine_kernel(where, mine, units, table, student, total, held, sems):
    half = held.shape[0]
    start = pl.multiple_of(where[0] * half, half)
    copies = [
        pltpu.make_async_copy(mine.at[:, pl.ds(0, D)], held, sems.at[0]),
        pltpu.make_async_copy(
            mine.at[:, pl.ds(D, D)], student.at[pl.ds(start, half), :], sems.at[1]
        ),
    ]
    for copy in copies:
        copy.start()
    copies[0].wait()
    exp_rows(held, start, units, table, total)
    copies[1].wait()


def exp_other_kernel(where, other, units, first, _, __, table, student, out, total):
    half = other.shape[0]
    start = pl.multiple_of((1 - where[0]) * half, half)
    student[pl.ds(start, half), :] = other[:, D:]
    exp_rows(other, start, units, table, total)
    every = first[...] + total[...]
    for k in range(out.shape[0]):
        out[k] = every


def col_scales(parts, scale):
    scale[...] = 1.0 / (PROTOS * jnp.sum(parts[...], axis=0))


def lane_sums(acc):
    ones = jnp.ones((8, LANES), F32)
    sums = lax.dot_general(
        ones, acc, (((1,), (1,)), ((), ())), precision=HIGHEST, preferred_element_type=F32
    )
    return sums[0:1, :]


def row_kernel(table, parts, out, scale, acc, total):
    col_scales(parts, scale)
    rows, cols = table.shape
    step = 64
    for i in range(0, rows, step):
        sums = jnp.zeros((step, LANES), F32)
        for j in range(cols // LANES):
            sums += table[i : i + step, j * LANES : (j + 1) * LANES] * scale[j : j + 1, :]
        acc[i : i + step, :] = sums
    col_rows(total, lane_sums(acc[...]), 0)
    every = total[...]
    for k in range(out.shape[0]):
        out[k] = every


def down(vector):
    return jnp.transpose(jnp.broadcast_to(vector, (LANES, LANES)))


def col_kernel(table, parts, out, weight, total):
    rows, cols = table.shape
    scale = 1.0 / (CROPS * jnp.sum(parts[...], axis=0))
    for t in range(rows // LANES):
        weight[t * LANES : (t + 1) * LANES, :] = down(scale[t : t + 1, :])
    tiles = 8
    for j in range(0, cols, tiles * LANES):
        sums = [jnp.zeros((8, LANES), F32) for _ in range(tiles)]
        for i in range(0, rows, 8):
            w = weight[i : i + 8, :]
            for t in range(tiles):
                sums[t] += table[i : i + 8, j + t * LANES : j + (t + 1) * LANES] * w
        for t in range(tiles):
            row = j // LANES + t
            total[row : row + 1, :] = jnp.sum(sums[t], axis=0, keepdims=True)
    every = total[...]
    for k in range(out.shape[0]):
        out[k] = every


def last_kernel(table, parts, student, units, out, scale, acc):
    col_scales(parts, scale)
    rows, cols = table.shape
    acc[...] = jnp.zeros_like(acc)
    width = 512
    step = 256
    for k in range(0, cols, width):
        for i in range(0, rows, step):
            z = jnp.dot(
                student[i : i + step, :], units[:D, k : k + width], preferred_element_type=F32
            )
            x = jnp.exp2(z * (STUDENT * LOG2E))
            plain = cross = exps = None
            for t in range(width // LANES):
                j = k // LANES + t
                here = slice(t * LANES, (t + 1) * LANES)
                e = table[i : i + step, j * LANES : (j + 1) * LANES] * scale[j : j + 1, :]
                zt, xt = z[:, here], x[:, here]
                plain = e if t == 0 else plain + e
                cross = e * zt if t == 0 else cross + e * zt
                exps = xt if t == 0 else exps + xt
            acc[0, i : i + step, :] += plain
            acc[1, i : i + step, :] += cross
            acc[2, i : i + step, :] += exps
    every = jnp.concatenate([lane_sums(acc[0]), lane_sums(acc[2])], axis=1)
    cross = lane_sums(acc[1]) * STUDENT
    count = out.shape[0]
    own = rows // count
    for k in range(count):
        tile = first_crop(k, rows // 2, own) // LANES
        out[k, :, : 2 * rows] = every
        out[k, :, 2 * rows :] = cross[:, tile * LANES : (tile + 1) * LANES]


def first_crop(number, half, own):
    return (number & 1) * half + (number >> 1) * own


def factor_kernel(where, parts, out, loss, sums):
    total = parts[0]
    for k in range(1, parts.shape[0]):
        total += parts[k]
    sums[...] = total
    rows = out.shape[2] // 2
    every = (LOSS_SCALE / 0.1) / total[:, : 2 * rows]
    for k in range(out.shape[0]):
        out[k] = every
    first = where[2]
    tile = pl.multiple_of(first // LANES * LANES, LANES)
    plain = sums[:, pl.ds(tile, LANES)]
    exps = sums[:, pl.ds(rows + tile, LANES)]
    row = jnp.log(exps) - total[:, 2 * rows :] / plain
    loss[...] = pltpu.roll(row, (LANES - first % LANES) % LANES, 1)[:, : loss.shape[1]]


def grad_kernel(
    order, where, mine, other, units, weight, inverse, scale, factors, own, out, loss,
    held, logits, wsub, punit, csub, turned, grad, sems, wsem, lsem,
):
    core, place = where[0], where[1]
    lcopy = pltpu.make_async_copy(own, loss, lsem)
    lcopy.start()
    groups = factors.shape[0]
    rows = factors.shape[2] // 2
    width = wsub.shape[1]
    half = mine.shape[0] // groups
    begin = pl.multiple_of(place * width, width)
    copies = []
    for n in range(groups):
        here = pl.ds(n * half, half)
        copies.append(pltpu.make_async_copy(mine.at[here, :], held.at[here, :], sems.at[n]))
        copies[-1].start()
    wcopy = pltpu.make_async_copy(weight.at[:, pl.ds(begin, width)], wsub, wsem)
    wcopy.start()
    punit[...] = jnp.transpose(units[:D, pl.ds(begin, width)])
    inv = inverse[:, pl.ds(begin, width)]
    tiles = width // LANES
    for t in range(tiles):
        csub[t * LANES : (t + 1) * LANES, :] = down(scale[pl.ds(place * tiles + t, 1), :])
    nt = (((1,), (1,)), ((), ()))
    last = 2 * groups

    def crops_of(c, here):
        n = c % groups
        return (other if c < groups else held)[n * half : (n + 1) * half, here]

    def products(c):
        for k in range(2):
            logits[c % 2, k] = lax.dot_general(
                punit[...], crops_of(c, slice(k * D, (k + 1) * D)), nt, preferred_element_type=F32
            )

    products(0)
    for c in range(last):
        if c + 1 == groups:
            for copy in copies:
                copy.wait()
        if c + 1 < last:
            products(c + 1)
        owner = 1 - core if c < groups else core
        group = order[c % groups]
        parts = []
        for t in range(0, half, LANES):
            at = pl.multiple_of(owner * half, half) + t
            a = factors[group, :, pl.ds(at, LANES)]
            b = factors[group, :, pl.ds(rows + at, LANES)]
            here = slice(t, t + LANES)
            x = jnp.exp2(logits[c % 2, 1, :, here] * (STUDENT * LOG2E)) * b
            e = jnp.exp2(logits[c % 2, 0, :, here] * TEACHER) * (csub[...] * a)
            parts.append((x - e).astype(BF16))
        part = jnp.dot(
            jnp.concatenate(parts, axis=1),
            crops_of(c, slice(D, 2 * D)),
            preferred_element_type=F32,
        )
        turned[...] = part if c == 0 else turned[...] + part
    for t in range(tiles):
        for d in range(0, D, LANES):
            grad[d : d + LANES, t * LANES : (t + 1) * LANES] = jnp.transpose(
                turned[t * LANES : (t + 1) * LANES, d : d + LANES]
            )
    wcopy.wait()
    inner = jnp.zeros((8, width), F32)
    for d in range(0, D, 8):
        inner += wsub[d : d + 8, :] * inv * grad[d : d + 8, :]
    inner = jnp.sum(inner, axis=0, keepdims=True)
    share = out.shape[1]
    for d in range(0, D, 8):
        cu = wsub[d : d + 8, :] * inv
        out[d // share, d % share : d % share + 8, :] = (grad[d : d + 8, :] - cu * inner) * inv
    lcopy.wait()


def struct(shape, dtype=F32):
    return jax.ShapeDtypeStruct(shape, dtype)


def local(teacher_feats, student_feats, proto_weight):
    crops, protos = lax.axis_size("crops"), lax.axis_size("protos")
    own = teacher_feats.shape[0]
    rows = own * protos
    half = rows // 2
    cols = proto_weight.shape[1]
    width = cols // crops
    share = D // crops
    ctile, rtile = cols // LANES, rows // LANES
    number = lax.axis_index("protos")
    place = lax.axis_index("crops")
    first = first_crop(number, half, own)
    where = jnp.stack([number & 1, place, first]).astype(jnp.int32)
    swap = [(j, j ^ 1) for j in range(protos)]
    group = [
        [
            (2 * y + (pair ^ (j >= protos // 2))) * protos + j
            for j in range(protos)
        ]
        for y in range(crops // 2)
        for pair in range(2)
    ]
    same_core = [g[core::2] for g in group for core in range(2)]
    both = ("crops", "protos")
    ring = list(range(0, crops, 2)) + list(range(crops - 1, 0, -2))

    def over_crops(x):
        return lax.all_to_all(x, "crops", 0, 0, tiled=True)

    def over_group(x):
        return lax.all_to_all(x, both, 0, 0, tiled=True, axis_index_groups=group)

    copies = pl.pallas_call(
        own_kernel,
        out_shape=pltpu.VMEM((protos // 2, own, 2 * D), BF16),
        in_specs=[HBM, HBM],
        out_specs=VMEM,
        scratch_shapes=[pltpu.VMEM((2, own, D), BF16), pltpu.SemaphoreType.DMA((2,))],
        compiler_params=params(),
        cost_estimate=cost(rows * D, 2 * rows * D),
    )(in_hbm(teacher_feats), in_hbm(student_feats))
    mine = lax.all_to_all(
        copies, both, 0, 0, tiled=True, axis_index_groups=same_core
    ).reshape(half, 2 * D)

    units, inverse = pl.pallas_call(
        prep_kernel,
        out_shape=(
            pltpu.VMEM((D + SPARE, cols), BF16),
            pltpu.VMEM((1, cols), F32),
        ),
        in_specs=[HBM],
        out_specs=(VMEM, VMEM),
        scratch_shapes=[pltpu.VMEM((8, D, cols // 8), F32), pltpu.SemaphoreType.DMA((8,))],
        compiler_params=params(),
        cost_estimate=cost(3 * D * cols, 4 * D * cols),
    )(in_hbm(proto_weight))
    mine, inverse, where = lax.optimization_barrier((mine, inverse, where))
    other = lax.ppermute(mine, "protos", swap)
    all_mine = lax.all_gather(mine, "crops", axis=0, tiled=True, axis_index_groups=[ring])

    table, student, total = pl.pallas_call(
        exp_mine_kernel,
        out_shape=(
            pltpu.VMEM((rows, cols), F32),
            pltpu.VMEM((rows, D), BF16),
            pltpu.VMEM((ctile, LANES), F32),
        ),
        in_specs=[SMEM, HBM, VMEM],
        out_specs=(VMEM, VMEM, VMEM),
        scratch_shapes=[pltpu.VMEM((half, D), BF16), pltpu.SemaphoreType.DMA((2,))],
        compiler_params=params(),
        cost_estimate=cost(rows * D * cols, 0, rows * cols // 2),
    )(where, in_hbm(mine), pinned(units))
    table, student, parts = pl.pallas_call(
        exp_other_kernel,
        out_shape=(
            pltpu.VMEM((rows, cols), F32),
            pltpu.VMEM((rows, D), BF16),
            struct((crops, ctile, LANES)),
        ),
        in_specs=[SMEM] + [VMEM] * 5,
        out_specs=(VMEM, VMEM, VMEM),
        input_output_aliases={4: 0, 5: 1},
        scratch_shapes=[pltpu.VMEM((ctile, LANES), F32)],
        compiler_params=params(),
        cost_estimate=cost(rows * D * cols, 0, rows * cols // 2),
    )(where, other, pinned(units), pinned(total), pinned(table), pinned(student))

    for step in range(2):
        rparts = pl.pallas_call(
            row_kernel,
            out_shape=struct((protos, rtile, LANES)),
            in_specs=[VMEM, VMEM],
            out_specs=VMEM,
            scratch_shapes=[
                pltpu.VMEM((ctile, LANES), F32),
                pltpu.VMEM((rows, LANES), F32),
                pltpu.VMEM((rtile, LANES), F32),
            ],
            compiler_params=params(),
            cost_estimate=cost(2 * rows * cols),
        )(pinned(table), over_crops(parts))
        parts = pl.pallas_call(
            col_kernel,
            out_shape=struct((crops, ctile, LANES)),
            in_specs=[VMEM, VMEM],
            out_specs=VMEM,
            scratch_shapes=[pltpu.VMEM((rows, LANES), F32), pltpu.VMEM((ctile, LANES), F32)],
            compiler_params=params(),
            cost_estimate=cost(2 * rows * cols),
        )(pinned(table), over_group(rparts))

    rparts, scale = pl.pallas_call(
        last_kernel,
        out_shape=(struct((protos, 1, 2 * rows + LANES)), struct((ctile, LANES))),
        in_specs=[VMEM, VMEM, VMEM, VMEM],
        out_specs=(VMEM, VMEM),
        scratch_shapes=[pltpu.VMEM((3, rows, LANES), F32)],
        compiler_params=params(),
        cost_estimate=cost(2 * rows * D * cols, 0, rows * cols),
    )(pinned(table), over_crops(parts), pinned(student), pinned(units))
    all_mine, rparts = lax.optimization_barrier((all_mine, rparts))
    all_other = lax.ppermute(all_mine, "protos", swap)
    factors, loss = pl.pallas_call(
        factor_kernel,
        out_shape=(pltpu.VMEM((crops, 1, 2 * rows), F32), pltpu.VMEM((1, own), F32)),
        in_specs=[SMEM, VMEM],
        out_specs=(VMEM, VMEM),
        scratch_shapes=[pltpu.VMEM((1, 2 * rows + LANES), F32)],
        compiler_params=params(),
    )(where, over_group(rparts))

    grad, loss = pl.pallas_call(
        functools.partial(grad_kernel, ring),
        out_shape=(pltpu.VMEM((crops, share, width), F32), pltpu.HBM((1, own), F32)),
        in_specs=[SMEM, HBM, VMEM, VMEM, HBM, VMEM, VMEM, VMEM, VMEM],
        out_specs=(VMEM, HBM),
        scratch_shapes=[
            pltpu.VMEM((crops * half, 2 * D), BF16),
            pltpu.VMEM((2, 2, width, half), F32),
            pltpu.VMEM((D, width), F32),
            pltpu.VMEM((width, D), BF16),
            pltpu.VMEM((width, LANES), F32),
            pltpu.VMEM((width, D), F32),
            pltpu.VMEM((D, width), F32),
            pltpu.SemaphoreType.DMA((crops,)),
            pltpu.SemaphoreType.DMA,
            pltpu.SemaphoreType.DMA,
        ],
        compiler_params=params(20),
        cost_estimate=cost(6 * CROPS * D * width, 0, 2 * CROPS * width),
    )(
        where, in_hbm(all_mine), pinned(all_other), pinned(units), in_hbm(proto_weight),
        pinned(inverse), scale, over_crops(factors), pinned(loss),
    )
    moved = over_crops(grad)
    weight_grad = moved.transpose(1, 0, 2).reshape(share, cols)
    return (weight_grad, loss.reshape(own))


def solution(mesh):
    placed = (P(("crops", "protos"), None), P(("crops", "protos"), None), P(None, "protos"))
    return jax.shard_map(
        local,
        mesh=mesh,
        in_specs=placed,
        out_specs=(P("crops", "protos"), P(("crops", "protos"))),
        check_vma=False,
    )
```

```python
import functools
import math

import jax
import jax.numpy as jnp
from jax import lax
from jax.experimental import pallas as pl
from jax.experimental.pallas import tpu as pltpu
from jax.sharding import PartitionSpec as P

D = 384
PROTOS = 131072
CROPS = 4096
LOSS_SCALE = 8192
LANES = 128
MIB = 1 << 20
F32 = jnp.float32
BF16 = jnp.bfloat16
SPARE = 16
HIGHEST = lax.Precision.HIGHEST
TEACHER = math.log2(math.e) / 0.07
STUDENT = 1.0 / 0.1
LOG2E = math.log2(math.e)
VMEM = pl.BlockSpec(memory_space=pltpu.VMEM)
HBM = pl.BlockSpec(memory_space=pltpu.HBM)


def params(mib=14):
    return pltpu.CompilerParams(vmem_limit_bytes=mib * MIB)


def pinned(x):
    return pltpu.with_memory_space_constraint(x, pltpu.VMEM)


def in_hbm(x):
    return pltpu.with_memory_space_constraint(x, pltpu.HBM)


def cost(flops=0, read=0, exps=0):
    return pl.CostEstimate(flops=int(flops), bytes_accessed=int(read), transcendentals=int(exps))


def unit(values):
    wide = values.astype(F32)
    return (wide * lax.rsqrt(jnp.sum(wide * wide, axis=1, keepdims=True) + 1e-6)).astype(BF16)


def own_kernel(teacher, student, out, held, sems):
    copies = [
        pltpu.make_async_copy(x, held.at[n], sems.at[n]) for n, x in enumerate((teacher, student))
    ]
    for copy in copies:
        copy.start()
    for copy in copies:
        copy.wait()
    rows = jnp.concatenate([unit(held[0]), unit(held[1])], axis=1)
    for k in range(out.shape[0]):
        out[k] = rows


def prep_kernel(weight, units, inverse, held, sems):
    blocks = held.shape[0]
    width = held.shape[2]
    copies = []
    for k in range(blocks):
        copy = pltpu.make_async_copy(weight.at[:, pl.ds(k * width, width)], held.at[k], sems.at[k])
        copy.start()
        copies.append(copy)
    for k in range(blocks):
        copies[k].wait()
        total = jnp.zeros((8, width), F32)
        for d in range(0, D, 8):
            part = held[k, d : d + 8, :]
            total += part * part
        inv = lax.rsqrt(jnp.sum(total, axis=0, keepdims=True) + 1e-6)
        inverse[:, k * width : (k + 1) * width] = inv
        for d in range(0, D, 16):
            units[d : d + 16, k * width : (k + 1) * width] = (held[k, d : d + 16, :] * inv).astype(BF16)

def col_rows(total, sums, start):
    for t in range(sums.shape[1] // LANES):
        total[start + t : start + t + 1, :] = sums[:, t * LANES : (t + 1) * LANES]


def exp_rows(rows, start, units, table, total):
    half = rows.shape[0]
    width = 512
    for k in range(table.shape[1] // width):
        cols = slice(k * width, (k + 1) * width)
        e = jnp.exp2(jnp.dot(rows[:, :D], units[:D, cols], preferred_element_type=F32) * TEACHER)
        table[pl.ds(start, half), cols] = e
        sums = e[0:8, :]
        for d in range(8, half, 8):
            sums += e[d : d + 8, :]
        col_rows(total, jnp.sum(sums, axis=0, keepdims=True), k * width // LANES)


def exp_mine_kernel(mine, units, table, student, total, held, sems):
    half = held.shape[0]
    start = pl.multiple_of((lax.axis_index("protos") & 1) * half, half)
    copies = [
        pltpu.make_async_copy(mine.at[:, pl.ds(0, D)], held, sems.at[0]),
        pltpu.make_async_copy(
            mine.at[:, pl.ds(D, D)], student.at[pl.ds(start, half), :], sems.at[1]
        ),
    ]
    for copy in copies:
        copy.start()
    copies[0].wait()
    exp_rows(held, start, units, table, total)
    copies[1].wait()


def exp_other_kernel(other, units, first, _, __, table, student, out, total):
    half = other.shape[0]
    start = pl.multiple_of((1 - (lax.axis_index("protos") & 1)) * half, half)
    student[pl.ds(start, half), :] = other[:, D:]
    exp_rows(other, start, units, table, total)
    every = first[...] + total[...]
    for k in range(out.shape[0]):
        out[k] = every


def col_scales(parts, scale):
    scale[...] = 1.0 / (PROTOS * jnp.sum(parts[...], axis=0))


def lane_sums(acc):
    ones = jnp.ones((8, LANES), F32)
    sums = lax.dot_general(
        ones, acc, (((1,), (1,)), ((), ())), precision=HIGHEST, preferred_element_type=F32
    )
    return sums[0:1, :]


def row_kernel(table, parts, out, scale, acc, total):
    col_scales(parts, scale)
    rows, cols = table.shape
    step = 64
    for i in range(0, rows, step):
        sums = jnp.zeros((step, LANES), F32)
        for j in range(cols // LANES):
            sums += table[i : i + step, j * LANES : (j + 1) * LANES] * scale[j : j + 1, :]
        acc[i : i + step, :] = sums
    col_rows(total, lane_sums(acc[...]), 0)
    every = total[...]
    for k in range(out.shape[0]):
        out[k] = every


def down(vector):
    return jnp.transpose(jnp.broadcast_to(vector, (LANES, LANES)))


def col_kernel(table, parts, out, weight, total):
    rows, cols = table.shape
    scale = 1.0 / (CROPS * jnp.sum(parts[...], axis=0))
    for t in range(rows // LANES):
        weight[t * LANES : (t + 1) * LANES, :] = down(scale[t : t + 1, :])
    tiles = 8
    for j in range(0, cols, tiles * LANES):
        sums = [jnp.zeros((8, LANES), F32) for _ in range(tiles)]
        for i in range(0, rows, 8):
            w = weight[i : i + 8, :]
            for t in range(tiles):
                sums[t] += table[i : i + 8, j + t * LANES : j + (t + 1) * LANES] * w
        for t in range(tiles):
            row = j // LANES + t
            total[row : row + 1, :] = jnp.sum(sums[t], axis=0, keepdims=True)
    every = total[...]
    for k in range(out.shape[0]):
        out[k] = every


def last_kernel(table, parts, student, units, out, scale, acc):
    col_scales(parts, scale)
    rows, cols = table.shape
    acc[...] = jnp.zeros_like(acc)
    width = 512
    step = 256
    for k in range(0, cols, width):
        for i in range(0, rows, step):
            z = jnp.dot(
                student[i : i + step, :], units[:D, k : k + width], preferred_element_type=F32
            )
            x = jnp.exp2(z * (STUDENT * LOG2E))
            plain = cross = exps = None
            for t in range(width // LANES):
                j = k // LANES + t
                here = slice(t * LANES, (t + 1) * LANES)
                e = table[i : i + step, j * LANES : (j + 1) * LANES] * scale[j : j + 1, :]
                zt, xt = z[:, here], x[:, here]
                plain = e if t == 0 else plain + e
                cross = e * zt if t == 0 else cross + e * zt
                exps = xt if t == 0 else exps + xt
            acc[0, i : i + step, :] += plain
            acc[1, i : i + step, :] += cross
            acc[2, i : i + step, :] += exps
    every = jnp.concatenate([lane_sums(acc[0]), lane_sums(acc[2])], axis=1)
    cross = lane_sums(acc[1]) * STUDENT
    count = out.shape[0]
    own = rows // count
    for k in range(count):
        tile = first_crop(k, rows // 2, own) // LANES
        out[k, :, : 2 * rows] = every
        out[k, :, 2 * rows :] = cross[:, tile * LANES : (tile + 1) * LANES]


def first_crop(number, half, own):
    return (number & 1) * half + (number >> 1) * own


def factor_kernel(parts, out, loss, sums):
    total = parts[0]
    for k in range(1, parts.shape[0]):
        total += parts[k]
    sums[...] = total
    rows = out.shape[2] // 2
    every = (LOSS_SCALE / 0.1) / total[:, : 2 * rows]
    for k in range(out.shape[0]):
        out[k] = every
    first = first_crop(lax.axis_index("protos"), rows // 2, loss.shape[1])
    tile = pl.multiple_of(first // LANES * LANES, LANES)
    plain = sums[:, pl.ds(tile, LANES)]
    exps = sums[:, pl.ds(rows + tile, LANES)]
    row = jnp.log(exps) - total[:, 2 * rows :] / plain
    loss[...] = pltpu.roll(row, (LANES - first % LANES) % LANES, 1)[:, : loss.shape[1]]


def grad_kernel(
    order, mine, other, units, weight, inverse, scale, factors, own, out, loss,
    held, logits, wsub, punit, csub, turned, grad, sems, wsem, lsem,
):
    core, place = lax.axis_index("protos") & 1, lax.axis_index("crops")
    lcopy = pltpu.make_async_copy(own, loss, lsem)
    lcopy.start()
    groups = factors.shape[0]
    rows = factors.shape[2] // 2
    width = wsub.shape[1]
    half = mine.shape[0] // groups
    begin = pl.multiple_of(place * width, width)
    copies = []
    for n in range(groups):
        here = pl.ds(n * half, half)
        copies.append(pltpu.make_async_copy(mine.at[here, :], held.at[here, :], sems.at[n]))
        copies[-1].start()
    wcopy = pltpu.make_async_copy(weight.at[:, pl.ds(begin, width)], wsub, wsem)
    wcopy.start()
    punit[...] = jnp.transpose(units[:D, pl.ds(begin, width)])
    inv = inverse[:, pl.ds(begin, width)]
    tiles = width // LANES
    for t in range(tiles):
        csub[t * LANES : (t + 1) * LANES, :] = down(scale[pl.ds(place * tiles + t, 1), :])
    nt = (((1,), (1,)), ((), ()))
    last = 2 * groups

    def crops_of(c, here):
        n = c % groups
        return (other if c < groups else held)[n * half : (n + 1) * half, here]

    def products(c):
        for k in range(2):
            logits[c % 2, k] = lax.dot_general(
                punit[...], crops_of(c, slice(k * D, (k + 1) * D)), nt, preferred_element_type=F32
            )

    products(0)
    for c in range(last):
        if c + 1 == groups:
            for copy in copies:
                copy.wait()
        if c + 1 < last:
            products(c + 1)
        owner = 1 - core if c < groups else core
        group = order[c % groups]
        parts = []
        for t in range(0, half, LANES):
            at = pl.multiple_of(owner * half, half) + t
            a = factors[group, :, pl.ds(at, LANES)]
            b = factors[group, :, pl.ds(rows + at, LANES)]
            here = slice(t, t + LANES)
            x = jnp.exp2(logits[c % 2, 1, :, here] * (STUDENT * LOG2E)) * b
            e = jnp.exp2(logits[c % 2, 0, :, here] * TEACHER) * (csub[...] * a)
            parts.append((x - e).astype(BF16))
        part = jnp.dot(
            jnp.concatenate(parts, axis=1),
            crops_of(c, slice(D, 2 * D)),
            preferred_element_type=F32,
        )
        turned[...] = part if c == 0 else turned[...] + part
    for t in range(tiles):
        for d in range(0, D, LANES):
            grad[d : d + LANES, t * LANES : (t + 1) * LANES] = jnp.transpose(
                turned[t * LANES : (t + 1) * LANES, d : d + LANES]
            )
    wcopy.wait()
    inner = jnp.zeros((8, width), F32)
    for d in range(0, D, 8):
        inner += wsub[d : d + 8, :] * inv * grad[d : d + 8, :]
    inner = jnp.sum(inner, axis=0, keepdims=True)
    share = out.shape[1]
    for d in range(0, D, 8):
        cu = wsub[d : d + 8, :] * inv
        out[d // share, d % share : d % share + 8, :] = (grad[d : d + 8, :] - cu * inner) * inv
    lcopy.wait()


def struct(shape, dtype=F32):
    return jax.ShapeDtypeStruct(shape, dtype)


def local(teacher_feats, student_feats, proto_weight):
    crops, protos = lax.axis_size("crops"), lax.axis_size("protos")
    own = teacher_feats.shape[0]
    rows = own * protos
    half = rows // 2
    cols = proto_weight.shape[1]
    width = cols // crops
    share = D // crops
    ctile, rtile = cols // LANES, rows // LANES
    swap = [(j, j ^ 1) for j in range(protos)]
    group = [
        [
            (2 * y + (pair ^ (j >= protos // 2))) * protos + j
            for j in range(protos)
        ]
        for y in range(crops // 2)
        for pair in range(2)
    ]
    same_core = [g[core::2] for g in group for core in range(2)]
    both = ("crops", "protos")
    ring = list(range(0, crops, 2)) + list(range(crops - 1, 0, -2))

    def over_crops(x):
        return lax.all_to_all(x, "crops", 0, 0, tiled=True)

    def over_group(x):
        return lax.all_to_all(x, both, 0, 0, tiled=True, axis_index_groups=group)

    copies = pl.pallas_call(
        own_kernel,
        out_shape=pltpu.VMEM((protos // 2, own, 2 * D), BF16),
        in_specs=[HBM, HBM],
        out_specs=VMEM,
        scratch_shapes=[pltpu.VMEM((2, own, D), BF16), pltpu.SemaphoreType.DMA((2,))],
        compiler_params=params(),
        cost_estimate=cost(rows * D, 2 * rows * D),
    )(in_hbm(teacher_feats), in_hbm(student_feats))
    mine = lax.all_to_all(
        copies, both, 0, 0, tiled=True, axis_index_groups=same_core
    ).reshape(half, 2 * D)

    units, inverse = pl.pallas_call(
        prep_kernel,
        out_shape=(
            pltpu.VMEM((D + SPARE, cols), BF16),
            pltpu.VMEM((1, cols), F32),
        ),
        in_specs=[HBM],
        out_specs=(VMEM, VMEM),
        scratch_shapes=[pltpu.VMEM((8, D, cols // 8), F32), pltpu.SemaphoreType.DMA((8,))],
        compiler_params=params(),
        cost_estimate=cost(3 * D * cols, 4 * D * cols),
    )(in_hbm(proto_weight))
    mine, inverse = lax.optimization_barrier((mine, inverse))
    other = lax.ppermute(mine, "protos", swap)
    all_mine = lax.all_gather(mine, "crops", axis=0, tiled=True, axis_index_groups=[ring])

    table, student, total = pl.pallas_call(
        exp_mine_kernel,
        out_shape=(
            pltpu.VMEM((rows, cols), F32),
            pltpu.VMEM((rows, D), BF16),
            pltpu.VMEM((ctile, LANES), F32),
        ),
        in_specs=[HBM, VMEM],
        out_specs=(VMEM, VMEM, VMEM),
        scratch_shapes=[pltpu.VMEM((half, D), BF16), pltpu.SemaphoreType.DMA((2,))],
        compiler_params=params(),
        cost_estimate=cost(rows * D * cols, 0, rows * cols // 2),
    )(in_hbm(mine), pinned(units))
    table, student, parts = pl.pallas_call(
        exp_other_kernel,
        out_shape=(
            pltpu.VMEM((rows, cols), F32),
            pltpu.VMEM((rows, D), BF16),
            struct((crops, ctile, LANES)),
        ),
        in_specs=[VMEM] * 5,
        out_specs=(VMEM, VMEM, VMEM),
        input_output_aliases={3: 0, 4: 1},
        scratch_shapes=[pltpu.VMEM((ctile, LANES), F32)],
        compiler_params=params(),
        cost_estimate=cost(rows * D * cols, 0, rows * cols // 2),
    )(other, pinned(units), pinned(total), pinned(table), pinned(student))

    for step in range(2):
        rparts = pl.pallas_call(
            row_kernel,
            out_shape=struct((protos, rtile, LANES)),
            in_specs=[VMEM, VMEM],
            out_specs=VMEM,
            scratch_shapes=[
                pltpu.VMEM((ctile, LANES), F32),
                pltpu.VMEM((rows, LANES), F32),
                pltpu.VMEM((rtile, LANES), F32),
            ],
            compiler_params=params(),
            cost_estimate=cost(2 * rows * cols),
        )(pinned(table), over_crops(parts))
        parts = pl.pallas_call(
            col_kernel,
            out_shape=struct((crops, ctile, LANES)),
            in_specs=[VMEM, VMEM],
            out_specs=VMEM,
            scratch_shapes=[pltpu.VMEM((rows, LANES), F32), pltpu.VMEM((ctile, LANES), F32)],
            compiler_params=params(),
            cost_estimate=cost(2 * rows * cols),
        )(pinned(table), over_group(rparts))

    rparts, scale = pl.pallas_call(
        last_kernel,
        out_shape=(struct((protos, 1, 2 * rows + LANES)), struct((ctile, LANES))),
        in_specs=[VMEM, VMEM, VMEM, VMEM],
        out_specs=(VMEM, VMEM),
        scratch_shapes=[pltpu.VMEM((3, rows, LANES), F32)],
        compiler_params=params(),
        cost_estimate=cost(2 * rows * D * cols, 0, rows * cols),
    )(pinned(table), over_crops(parts), pinned(student), pinned(units))
    all_mine, rparts = lax.optimization_barrier((all_mine, rparts))
    all_other = lax.ppermute(all_mine, "protos", swap)
    factors, loss = pl.pallas_call(
        factor_kernel,
        out_shape=(pltpu.VMEM((crops, 1, 2 * rows), F32), pltpu.VMEM((1, own), F32)),
        in_specs=[VMEM],
        out_specs=(VMEM, VMEM),
        scratch_shapes=[pltpu.VMEM((1, 2 * rows + LANES), F32)],
        compiler_params=params(),
    )(over_group(rparts))

    grad, loss = pl.pallas_call(
        functools.partial(grad_kernel, ring),
        out_shape=(pltpu.VMEM((crops, share, width), F32), pltpu.HBM((1, own), F32)),
        in_specs=[HBM, VMEM, VMEM, HBM, VMEM, VMEM, VMEM, VMEM],
        out_specs=(VMEM, HBM),
        scratch_shapes=[
            pltpu.VMEM((crops * half, 2 * D), BF16),
            pltpu.VMEM((2, 2, width, half), F32),
            pltpu.VMEM((D, width), F32),
            pltpu.VMEM((width, D), BF16),
            pltpu.VMEM((width, LANES), F32),
            pltpu.VMEM((width, D), F32),
            pltpu.VMEM((D, width), F32),
            pltpu.SemaphoreType.DMA((crops,)),
            pltpu.SemaphoreType.DMA,
            pltpu.SemaphoreType.DMA,
        ],
        compiler_params=params(20),
        cost_estimate=cost(6 * CROPS * D * width, 0, 2 * CROPS * width),
    )(
        in_hbm(all_mine), pinned(all_other), pinned(units), in_hbm(proto_weight),
        pinned(inverse), scale, over_crops(factors), pinned(loss),
    )
    moved = over_crops(grad)
    weight_grad = moved.transpose(1, 0, 2).reshape(share, cols)
    return (weight_grad, loss.reshape(own))


def solution(mesh):
    placed = (P(("crops", "protos"), None), P(("crops", "protos"), None), P(None, "protos"))
    return jax.shard_map(
        local,
        mesh=mesh,
        in_specs=placed,
        out_specs=(P("crops", "protos"), P(("crops", "protos"))),
        check_vma=False,
    )
```
